32 devices in a mesh: blk: 8 (over y, x, core), dp: 4 (over z).
Axes of the slice: x: 2, y: 2, z: 4, core: 2. Of those that a mesh axis runs over, the one named last changes fastest.
Arguments:
- hidden_in: bfloat16 [16384, 8192], P(('blk', 'dp')), may hold values from -6 to 6
- segment_ids: int32 [64, 256], P(('blk', 'dp')), may hold values from 0 to 3, never falling along the last dimension, each value on 1 to 128 neighbouring positions
- key_weight: bfloat16 [8192, 512], P('blk'), may hold values from -0.0625 to 0.0625
- norm_gain: float32 [8192], replicated, may hold values from 0.5 to 1.5
- key_bias: float32 [512], replicated, may hold values from -6 to 6
- key_cotangent: bfloat16 [16384, 512], P(('blk', 'dp')), may hold values from -6 to 6
Outputs:
- keys: bfloat16 [16384, 512], P(('blk', 'dp'))
- grad_weight: float32 [8192, 512], P('blk')
- grad_bias: float32 [512], replicated
- grad_gain: float32 [8192], replicated
The draws below stay inside these ranges and needn't reach their ends.
Inputs may be any that keep to these rules, and one draw needn't show every extreme that they name: `segment_ids`: segment ids never fall along a micro-batch; each segment has 1 to 128 tokens.
All inputs are finite; a program needn't handle non-finite values.
Results may differ from the reference program's by a relative error of at most 0.0048.
Values may be sent and summed in bfloat16 or wider, within the bound.
No kernel may reach another device: no remote copies, remote signals or barrier semaphores. Data moves between devices by JAX's collectives and lax.ppermute only.
A program may use at most 128 MiB of HBM per device.

```python
import math
import jax
import jax.numpy as jnp
import numpy as np
from jax import lax

D = 8192
KVH = 4
HEAD = 128
SEQ = 256
KW = 512
MBALL = 64
ALL_TOKENS = 16384


def raised(result, key, source, target, blocks, factor):
    def block_of(axis_at):
        return (jnp.arange(result.shape[axis_at]) // (result.shape[axis_at] // blocks)).reshape((-1,) + (1,) * (result.ndim - 1 - axis_at))

    one_side = jax.random.permutation(key, blocks)[block_of(target)]
    second = (block_of(target) + blocks // 2) % blocks
    return jnp.where((block_of(source) == one_side) | (block_of(source) == second), factor * result, result)


def shard_levels(stream_key, dims, shards, low, largest):
    def one(dim, shards_of):
        draws = jax.random.uniform(jax.random.fold_in(jax.random.fold_in(stream_key, 6), dim), (shards_of,), jnp.float32, low / len(shards), largest / len(shards))
        return jnp.repeat(jnp.exp(draws), dims[dim] // shards_of).reshape((-1,) + (1,) * (len(dims) - dim - 1))

    factor_of = one(*shards[0])
    for cut in shards[1:]:
        factor_of = factor_of * one(*cut)
    return factor_of


def split_up(amount, total, bound, slope):
    loads = [(1 << 20) // math.isqrt(rank ** slope) + 1 for rank in range(2, amount + 1)]
    surplus, holding = total - bound - (amount - 1), [1] * (amount - 1)
    while surplus > 0:
        free = [i for i in range(amount - 1) if holding[i] < bound]
        pool, remaining = sum([loads[i] for i in free]), surplus
        for i in free:
            addition = min(bound - holding[i], max(1, remaining * loads[i] // pool), surplus)
            holding[i] = holding[i] + addition
            surplus = surplus - addition
    return np.array([bound] + holding)


def ragged_sizes(key, amount, total, reach, skew):
    if amount == 2:
        one = jax.random.randint(key, (), max(1, total - reach), min(reach, total - 1) + 1)
        return jnp.stack([one, total - one])
    lengths = jnp.asarray(split_up(amount, total, reach, skew), jnp.int32)
    pairs = (amount - 1) // 2
    donor, receiver = lengths[1:1 + 2 * pairs:2], lengths[2:2 + 2 * pairs:2]
    room = jnp.minimum(donor - 1, reach - receiver)
    passed = jax.random.randint(jax.random.fold_in(key, 1), (pairs,), 0, 1 << 20) % (room + 1)
    lengths = lengths.at[1:1 + 2 * pairs:2].set(donor - passed).at[2:2 + 2 * pairs:2].set(receiver + passed)
    return lengths[jax.random.permutation(jax.random.fold_in(key, 2), amount)]


def bell_draw(key, dims, spread, bound, pieces=(), held_as=jnp.bfloat16):
    loudness = shard_levels(key, dims, pieces, -0.22, 0.18) if pieces else 1.0
    drawn = jax.random.normal(key, dims, jnp.float32) * spread * loudness
    return jnp.minimum(jnp.maximum(drawn, -bound), bound).astype(held_as)


def bell_draw_with(own_key, extent, scale, bound, split, heavy, held_as=jnp.bfloat16):
    drawn = scale * jax.random.normal(own_key, extent, jnp.float32)
    if split:
        drawn = drawn * shard_levels(own_key, extent, split, -0.22, 0.18)
    return jnp.clip(raised(drawn, jax.random.fold_in(own_key, 3), *heavy), -bound, bound).astype(held_as)


def setup_inputs(seed: int = 0) -> dict:
    key_of = jax.random.split(jax.random.key(seed), 7)
    hidden_in = bell_draw_with(key_of[0], (ALL_TOKENS, D), 1.0, 6.0, ((0, 32),), (0, 1, 32, 2.75))
    segment_ids = jax.vmap(lambda own: jnp.searchsorted(jnp.cumsum(ragged_sizes(own, 4, SEQ, SEQ // 2, 0)), jnp.arange(SEQ), side="right"))(jax.random.split(key_of[1], MBALL)).reshape((MBALL, SEQ)).astype(jnp.int32)
    key_weight = bell_draw(key_of[2], (D, KW), D ** -0.5, 0.0625, ((0, 8),))
    norm_gain = jnp.clip(1.0 + 0.1 * jax.random.normal(key_of[3], (D,), jnp.float32), 0.5, 1.5)
    key_bias = bell_draw(key_of[4], (KW,), 1.0, 6.0, (), jnp.float32)
    key_cotangent = bell_draw(key_of[5], (ALL_TOKENS, KW), 1.0, 6.0, ((0, 32),))
    return {"hidden_in": hidden_in, "segment_ids": segment_ids, "key_weight": key_weight, "norm_gain": norm_gain, "key_bias": key_bias, "key_cotangent": key_cotangent}


def positions_of(segs):
    same = segs[:, :, None] == segs[:, None, :]
    idx = jnp.arange(segs.shape[1], dtype=jnp.int32)
    earlier = idx[None, :] < idx[:, None]
    return lax.optimization_barrier(jnp.sum((same & earlier[None]).astype(jnp.int32), axis=2)).astype(jnp.int32)

def angles_of(pos, head):
    half = head // 2
    freq = jnp.arange(half, dtype=jnp.float32) * (2.0 / head)
    inv = jnp.power(jnp.float32(1000000.0), -freq)
    ang = pos.astype(jnp.float32)[:, None] * inv[None, :]
    return (jnp.cos(ang)[:, None, :], jnp.sin(ang)[:, None, :])

def rotate(values, cosine, sine, sign):
    rows = values.shape[0]
    heads = values.reshape(rows, KVH, HEAD)
    first = heads[:, :, :HEAD // 2]
    second = heads[:, :, HEAD // 2:]
    out_a = first * cosine - sign * second * sine
    out_b = second * cosine + sign * first * sine
    return jnp.concatenate([out_a, out_b], axis=2).reshape(rows, KW)

def reference(hidden_in, segment_ids, key_weight, norm_gain, key_bias, key_cotangent):
    pos_all = positions_of(segment_ids).reshape(MBALL, SEQ)
    xs = hidden_in.reshape(MBALL, SEQ, D)
    cots = key_cotangent.reshape(MBALL, SEQ, KW)

    def step(carry, item):
        gw, gb, gg = carry
        rows, pos, cot = item
        xf = rows.astype(jnp.float32)
        normed = xf * lax.rsqrt(lax.optimization_barrier(jnp.mean(xf * xf, axis=1, keepdims=True)) + 1e-06)
        scaled = (normed * norm_gain[None, :]).astype(jnp.bfloat16)
        projected = jnp.dot(scaled, key_weight, preferred_element_type=jnp.float32) + key_bias[None, :]
        cosine, sine = angles_of(pos, HEAD)
        keys = rotate(projected, cosine, sine, 1.0).astype(jnp.bfloat16)
        dproj = rotate(cot.astype(jnp.float32), cosine, sine, -1.0).astype(jnp.bfloat16)
        gw = gw + jnp.dot(scaled.T, dproj, preferred_element_type=jnp.float32)
        gb = gb + lax.optimization_barrier(jnp.sum(dproj.astype(jnp.float32), axis=0))
        dscaled = jnp.dot(dproj, key_weight.T, preferred_element_type=jnp.float32)
        gg = gg + lax.optimization_barrier(jnp.sum(dscaled * normed, axis=0))
        return ((gw, gb, gg), keys)
    init = (jnp.zeros((D, KW), jnp.float32), jnp.zeros((KW,), jnp.float32), jnp.zeros((D,), jnp.float32))
    (gw, gb, gg), keys = lax.scan(step, init, (xs, pos_all, cots))
    scale = 1.0 / jnp.sqrt(jnp.float32(ALL_TOKENS))
    return (keys.reshape(ALL_TOKENS, KW), gw * scale, gb * scale, gg * scale)
```

```python
import functools

import jax
import jax.numpy as jnp
from jax import lax
from jax.experimental import pallas as pl
from jax.experimental.pallas import tpu as pltpu
from jax.sharding import PartitionSpec as P

KVH = 4
HEAD = 128
KW = 512
F32 = jnp.float32
BF16 = jnp.bfloat16


def positions_of(segs):
    same = segs[:, :, None] == segs[:, None, :]
    idx = jnp.arange(segs.shape[1], dtype=jnp.int32)
    earlier = idx[None, :] < idx[:, None]
    return jnp.sum((same & earlier[None]).astype(jnp.int32), axis=2)


def angles_of(pos, head):
    half = head // 2
    freq = jnp.arange(half, dtype=F32) * (2.0 / head)
    inv = jnp.power(F32(1000000.0), -freq)
    ang = pos.astype(F32)[:, None] * inv[None, :]
    return (jnp.cos(ang)[:, None, :], jnp.sin(ang)[:, None, :])


def rotate(values, cosine, sine, sign):
    rows = values.shape[0]
    heads = values.reshape(rows, KVH, HEAD)
    first = heads[:, :, : HEAD // 2]
    second = heads[:, :, HEAD // 2 :]
    out_a = first * cosine - sign * second * sine
    out_b = second * cosine + sign * first * sine
    return jnp.concatenate([out_a, out_b], axis=2).reshape(rows, KW)


def scale_body(n_blk, at_ref, x_ref, gain_ref, *outs):
    wide = x_ref.shape[1]
    part = wide // n_blk
    total = None
    for b in range(n_blk):
        xb = x_ref[:, b * part : (b + 1) * part].astype(F32)
        add = jnp.sum(xb * xb, axis=1, keepdims=True)
        total = add if total is None else total + add
    inv = lax.rsqrt(total * (1.0 / wide) + 1e-06)
    me = at_ref[0]
    for o, out in enumerate(outs):
        start = pl.multiple_of((me ^ o) * part, part)
        xb = x_ref[:, pl.ds(start, part)].astype(F32)
        out[...] = (xb * inv * gain_ref[:, pl.ds(start, part)]).astype(BF16)


def scaled_blocks(x, gain, n_blk, at):
    rows, wide = x.shape
    step = 64
    part = wide // n_blk
    return pl.pallas_call(
        functools.partial(scale_body, n_blk),
        grid_spec=pltpu.PrefetchScalarGridSpec(
            num_scalar_prefetch=1,
            grid=(rows // step,),
            in_specs=[
                pl.BlockSpec((step, wide), lambda r, at: (r, 0)),
                pl.BlockSpec((1, wide), lambda r, at: (0, 0)),
            ],
            out_specs=[pl.BlockSpec((step, part), lambda r, at: (r, 0))] * n_blk,
        ),
        out_shape=[jax.ShapeDtypeStruct((rows, part), BF16)] * n_blk,
        cost_estimate=pl.CostEstimate(
            flops=6 * rows * wide, bytes_accessed=4 * rows * wide, transcendentals=rows
        ),
        compiler_params=pltpu.CompilerParams(vmem_limit_bytes=16 * 1024 * 1024),
        name="scale_rows",
    )(at, x, gain[None, :])


def by_permutes(hidden_in, segment_ids, key_weight, norm_gain, key_bias, key_cotangent):
    tok = hidden_in.shape[0]
    me = lax.axis_index("blk")
    own = key_weight.shape[0]
    half = own // 2

    def over(bit):
        return lambda v: lax.ppermute(v, "blk", [(i, i ^ bit) for i in range(8)])

    core, px, py = over(1), over(2), over(4)

    def dot_t(a, b):
        return lax.dot_general(a, b, (((0,), (0,)), ((), ())), preferred_element_type=F32)

    def dot(a, b):
        return jnp.dot(a, b, preferred_element_type=F32)

    w_x, w_y = px(key_weight), py(key_weight)
    w_d = jnp.concatenate([px(w_y[:half]), py(w_x[half:])], axis=0)

    positions = positions_of(segment_ids).reshape(tok)
    cosine, sine = angles_of(positions, HEAD)
    dproj = rotate(key_cotangent.astype(F32), cosine, sine, -1.0).astype(BF16)
    dproj_sib = core(dproj)

    blocks = scaled_blocks(hidden_in, norm_gain, 8, me.reshape(1).astype(jnp.int32))
    mine = {j: blocks[j] for j in (0, 2, 4, 6)}
    sib = {j: core(blocks[j ^ 1]) for j in (6, 2, 4, 0)}

    def grad_rows(j):
        return dot_t(mine[j], dproj) + dot_t(sib[j], dproj_sib)

    g_d = grad_rows(6).astype(BF16)
    d_x, d_y = px(g_d[:half]), py(g_d[half:])
    g_x = grad_rows(2).astype(BF16)
    g_y = grad_rows(4).astype(BF16)
    x_low, y_high = px(g_x[:half]), py(g_y[half:])
    x_high = px((g_x[half:].astype(F32) + d_y.astype(F32)).astype(BF16))
    y_low = py((g_y[:half].astype(F32) + d_x.astype(F32)).astype(BF16))
    g_0 = grad_rows(0)

    n_z = lax.axis_index("dp")
    inner = (n_z == 1) | (n_z == 2)

    def along_z(g):
        into = lax.ppermute(g.astype(BF16), "dp", [(0, 1), (3, 2)])
        pair = (g + into.astype(F32)).astype(BF16)
        other = lax.ppermute(pair, "dp", [(1, 2), (2, 1)])
        total = (pair.astype(F32) + other.astype(F32)).astype(BF16)
        back = lax.ppermute(total, "dp", [(1, 0), (2, 3)])
        return jnp.where(inner, total, back).astype(F32)

    low = g_0[:half] + x_low.astype(F32) + y_low.astype(F32)
    high = g_0[half:] + x_high.astype(F32) + y_high.astype(F32)
    quarter = half // 2
    done = [along_z(v) for v in (low[:quarter], low[quarter:], high[:quarter], high[quarter:])]
    grad = jnp.concatenate(done, axis=0)

    here = dot(mine[0], key_weight) + dot(mine[2], w_x) + dot(mine[4], w_y) + dot(mine[6], w_d)
    there = dot(sib[0], key_weight) + dot(sib[2], w_x) + dot(sib[4], w_y) + dot(sib[6], w_d)
    projected = here + core(there) + key_bias[None, :]
    keys = rotate(projected, cosine, sine, 1.0).astype(BF16)

    scale = 1.0 / jnp.sqrt(F32(tok * 32))
    bias = jnp.sum(dproj.astype(F32), axis=0)
    for hop in (core, px, py):
        bias = bias + hop(bias)
    for bit in (1, 2):
        bias = bias + lax.ppermute(bias, "dp", [(i, i ^ bit) for i in range(4)])
    my_gain = lax.dynamic_slice(norm_gain, (me * own,), (own,))
    gain_rows = jnp.sum(grad * key_weight.astype(F32), axis=1) / my_gain
    grad_gain = lax.all_gather(gain_rows, "blk", axis=0, tiled=True)
    return (keys, grad * scale, bias * scale, grad_gain * scale)


def by_collectives(hidden_in, segment_ids, key_weight, norm_gain, key_bias, key_cotangent):
    tok_rows = hidden_in.shape[0]
    n_cycle = lax.axis_size("blk")
    n_rep = lax.axis_size("dp")
    positions = positions_of(segment_ids).reshape(tok_rows)
    xf = hidden_in.astype(F32)
    normed = xf * lax.rsqrt(jnp.mean(xf * xf, axis=1, keepdims=True) + 1e-06)
    scaled = (normed * norm_gain[None, :]).astype(BF16)
    cosine, sine = angles_of(positions, HEAD)
    dproj = rotate(key_cotangent.astype(F32), cosine, sine, -1.0).astype(BF16)
    full_weight = lax.all_gather(key_weight, "blk", axis=0, tiled=True)
    projected = jnp.dot(scaled, full_weight, preferred_element_type=F32)
    dscaled = lax.dot_general(
        dproj, full_weight, (((1,), (1,)), ((), ())), preferred_element_type=F32
    )
    projected = projected + key_bias[None, :]
    keys = rotate(projected, cosine, sine, 1.0).astype(BF16)
    cycle_part = lax.psum_scatter(
        lax.dot_general(scaled, dproj, (((0,), (0,)), ((), ())), preferred_element_type=F32),
        "blk",
        scatter_dimension=0,
        tiled=True,
    )
    grad_weight = lax.psum(cycle_part, "dp")
    bias_part = jnp.sum(dproj.astype(F32), axis=0)
    gain_part = jnp.sum(dscaled * normed, axis=0)
    grad_bias, grad_gain = lax.psum((bias_part, gain_part), ("blk", "dp"))
    scale = 1.0 / jnp.sqrt(F32(tok_rows * n_cycle * n_rep))
    return (keys, grad_weight * scale, grad_bias * scale, grad_gain * scale)


def solution(mesh):
    small = mesh.shape["blk"] == 8 and mesh.shape["dp"] == 4
    return jax.shard_map(
        by_permutes if small else by_collectives,
        mesh=mesh,
        in_specs=(
            P(("blk", "dp"), None),
            P(("blk", "dp"), None),
            P("blk", None),
            P(),
            P(),
            P(("blk", "dp"), None),
        ),
        out_specs=(P(("blk", "dp"), None), P("blk", None), P(), P()),
        check_vma=False,
    )
```

```python
import functools

import jax
import jax.numpy as jnp
from jax import lax
from jax.experimental import pallas as pl
from jax.experimental.pallas import tpu as pltpu
from jax.sharding import PartitionSpec as P

KVH = 4
HEAD = 128
KW = 512
F32 = jnp.float32
BF16 = jnp.bfloat16


def positions_of(segs):
    same = segs[:, :, None] == segs[:, None, :]
    idx = jnp.arange(segs.shape[1], dtype=jnp.int32)
    earlier = idx[None, :] < idx[:, None]
    return jnp.sum((same & earlier[None]).astype(jnp.int32), axis=2)


def angles_of(pos, head):
    half = head // 2
    freq = jnp.arange(half, dtype=F32) * (2.0 / head)
    inv = jnp.power(F32(1000000.0), -freq)
    ang = pos.astype(F32)[:, None] * inv[None, :]
    return (jnp.cos(ang)[:, None, :], jnp.sin(ang)[:, None, :])


def rotate(values, cosine, sine, sign):
    rows = values.shape[0]
    heads = values.reshape(rows, KVH, HEAD)
    first = heads[:, :, : HEAD // 2]
    second = heads[:, :, HEAD // 2 :]
    out_a = first * cosine - sign * second * sine
    out_b = second * cosine + sign * first * sine
    return jnp.concatenate([out_a, out_b], axis=2).reshape(rows, KW)


def call(body, out_shape, flops, nbytes, name):
    return pl.pallas_call(
        body,
        out_shape=out_shape,
        cost_estimate=pl.CostEstimate(flops=flops, bytes_accessed=nbytes, transcendentals=0),
        compiler_params=pltpu.CompilerParams(vmem_limit_bytes=16 * 1024 * 1024),
        name=name,
    )


def after(value, *others):
    return lax.optimization_barrier((value, *others))[0]


def scale_body(at_ref, x_ref, gain_ref, mine_a, mine_b, sib_a, sib_b):
    wide = x_ref.shape[1]
    part = wide // 8
    quarter = part // 4
    total = None
    for b in range(8):
        xb = x_ref[:, b * part : (b + 1) * part].astype(F32)
        add = jnp.sum(xb * xb, axis=1, keepdims=True)
        total = add if total is None else total + add
    inv = lax.rsqrt(total * (1.0 / wide) + 1e-06)
    me = at_ref[0]
    for o in range(8):
        start = pl.multiple_of((me ^ o) * part, part)
        outs = (sib_a, sib_b) if o & 1 else (mine_a, mine_b)
        for q in range(4):
            cols = pl.ds(start + q * quarter, quarter)
            xb = x_ref[:, cols].astype(F32)
            to = (o // 2 * 2 + q // 2) * quarter
            outs[q % 2][:, to : to + quarter] = (xb * inv * gain_ref[:, cols]).astype(BF16)


def scaled_parts(x, gain, at):
    rows, wide = x.shape
    step = 64
    part = wide // 4
    return pl.pallas_call(
        scale_body,
        grid_spec=pltpu.PrefetchScalarGridSpec(
            num_scalar_prefetch=1,
            grid=(rows // step,),
            in_specs=[
                pl.BlockSpec((step, wide), lambda r, at: (r, 0)),
                pl.BlockSpec((1, wide), lambda r, at: (0, 0)),
            ],
            out_specs=[pl.BlockSpec((step, part), lambda r, at: (r, 0))] * 4,
        ),
        out_shape=[jax.ShapeDtypeStruct((rows, part), BF16)] * 4,
        cost_estimate=pl.CostEstimate(
            flops=6 * rows * wide, bytes_accessed=4 * rows * wide, transcendentals=rows
        ),
        compiler_params=pltpu.CompilerParams(vmem_limit_bytes=44 * 1024 * 1024),
        name="scale_rows",
    )(at, x, gain[None, :])


def grad_body(mine, sib, dproj, dproj_sib, to_x, to_y, keep_y, keep_x, own_low, own_high):
    quarter = mine.shape[1] // 8
    extra = own_low.shape[0] - quarter

    def rows(chip, high):
        at = (2 * chip + high) * quarter
        dims = (((0,), (0,)), ((), ()))
        return lax.dot_general(
            mine[:, at : at + quarter], dproj[...], dims, preferred_element_type=F32
        ) + lax.dot_general(
            sib[:, at : at + quarter], dproj_sib[...], dims, preferred_element_type=F32
        )

    if extra:
        bias = jnp.sum(dproj[...].astype(F32), axis=0, keepdims=True) + jnp.sum(
            dproj_sib[...].astype(F32), axis=0, keepdims=True
        )
        first = lax.broadcasted_iota(jnp.int32, (extra, 1), 0) == 0
        below = jnp.where(first, bias, 0.0)
    low = quarter + extra
    for chip, ref, at in ((1, to_x, 0), (3, to_x, low), (2, keep_y, 0), (0, own_low, 0)):
        ref[at : at + quarter] = rows(chip, 0).astype(ref.dtype)
        if extra:
            ref[at + quarter : at + low] = below.astype(ref.dtype)
    for chip, ref, at in ((2, to_y, 0), (3, to_y, quarter), (1, keep_x, 0), (0, own_high, 0)):
        ref[at : at + quarter] = rows(chip, 1).astype(ref.dtype)


def grad_parts(mine, sib, dproj, dproj_sib, extra):
    tok, wide = mine.shape
    q = wide // 8
    low = q + extra
    kw = dproj.shape[1]
    shapes = ((2 * low, BF16), (2 * q, BF16), (low, BF16), (q, BF16), (low, F32), (q, F32))
    return call(
        grad_body,
        [jax.ShapeDtypeStruct((r, kw), t) for r, t in shapes],
        4 * tok * wide * kw,
        4 * tok * wide + 2 * wide * kw,
        "grad_rows",
    )(mine, sib, dproj, dproj_sib)


def forward_body(places, n_init, *refs):
    acts, refs = refs[:4], refs[4:]
    init, weights, outs = refs[:n_init], refs[n_init:-2], refs[-2:]
    quarter = acts[0].shape[1] // 8
    for side, out in enumerate(outs):
        total = init[side][...] if n_init else None
        for (chip, high), w in zip(places, weights, strict=True):
            for chunk in (0, 1):
                at = (2 * chip + high) * quarter
                add = jnp.dot(
                    acts[2 * side + chunk][:, at : at + quarter],
                    w[chunk * quarter : (chunk + 1) * quarter],
                    preferred_element_type=F32,
                )
                total = add if total is None else total + add
        out[...] = total


def forward(acts, places, weights, init=()):
    tok = acts[0].shape[0]
    rows, kw = weights[0].shape
    return call(
        functools.partial(forward_body, places, len(init)),
        [jax.ShapeDtypeStruct((tok, kw), F32)] * 2,
        4 * tok * rows * kw * len(weights),
        4 * tok * rows * len(weights) + 8 * tok * kw,
        "forward",
    )(*acts, *init, *weights)


def by_permutes(hidden_in, segment_ids, key_weight, norm_gain, key_bias, key_cotangent):
    tok = hidden_in.shape[0]
    me = lax.axis_index("blk")
    own = key_weight.shape[0]
    half = own // 2
    quarter = own // 4

    def over(bit):
        return lambda v: lax.ppermute(v, "blk", [(i, i ^ bit) for i in range(8)])

    core, px, py = over(1), over(2), over(4)

    w_low, w_high = key_weight[:half], key_weight[half:]
    wy_low, wx_high = py(w_low), px(w_high)

    positions = positions_of(segment_ids).reshape(tok)
    cosine, sine = angles_of(positions, HEAD)
    dproj = rotate(key_cotangent.astype(F32), cosine, sine, -1.0).astype(BF16)
    dproj_sib = core(dproj)

    mine_a, mine_b, send_a, send_b = scaled_parts(
        hidden_in, norm_gain, me.reshape(1).astype(jnp.int32)
    )
    sib_a, sib_b = core(send_a), core(send_b)
    acts = (mine_a, mine_b, sib_a, sib_b)

    def widen(v):
        return v.astype(F32)

    def phase_one(parts):
        to_x, to_y, keep_y, keep_x, own_low, own_high = parts
        from_x, from_y = px(to_x), py(to_y)
        low = own_low.shape[0]
        more_y = (widen(keep_y) + widen(from_x[low:])).astype(BF16)
        more_x = (widen(keep_x) + widen(from_y[quarter:])).astype(BF16)
        return more_y, more_x, own_low + widen(from_x[:low]), own_high + widen(from_y[:quarter])

    n_z = lax.axis_index("dp")
    inner = (n_z == 1) | (n_z == 2)

    def along_z(g):
        into = lax.ppermute(g.astype(BF16), "dp", [(0, 1), (3, 2)])
        pair = (g + widen(into)).astype(BF16)
        other = lax.ppermute(pair, "dp", [(1, 2), (2, 1)])
        total = (widen(pair) + widen(other)).astype(BF16)
        back = lax.ppermute(total, "dp", [(1, 0), (2, 3)])
        return widen(jnp.where(inner, total, back))

    def phase_two(more_y, more_x, low, high):
        return along_z(low + widen(py(more_y))), along_z(high + widen(px(more_x)))

    part_a = grad_parts(mine_a, sib_a, dproj, dproj_sib, 16)
    one_a = phase_one(part_a)
    part_b = grad_parts(after(mine_b, part_a), sib_b, dproj, dproj_sib, 0)
    one_b = phase_one(part_b)

    own_w = after((w_low, w_high), part_b)
    here = forward(acts, ((0, 0), (0, 1), (2, 0), (1, 1)), (*own_w, wy_low, wx_high))
    low_a, high_a = phase_two(*one_a)
    later = after((w_low, w_high, wy_low, wx_high), one_a)
    wx_low, wy_high = px(later[0]), py(later[1])
    wd_low, wd_high = px(later[2]), py(later[3])
    low_b, high_b = phase_two(*one_b)

    here, there = forward(
        acts, ((1, 0), (2, 1), (3, 0), (3, 1)), (wx_low, wy_high, wd_low, wd_high), here
    )
    projected = here + core(there) + key_bias[None, :]
    keys = rotate(projected, cosine, sine, 1.0).astype(BF16)

    scale = 1.0 / jnp.sqrt(F32(tok * 32))
    grad = jnp.concatenate([low_a[:quarter], low_b, high_a, high_b], axis=0)
    bias = low_a[quarter]
    my_gain = lax.dynamic_slice(norm_gain, (me * own,), (own,))
    gain_rows = jnp.sum(grad * widen(key_weight), axis=1) / my_gain
    grad_gain = lax.all_gather(gain_rows, "blk", axis=0, tiled=True)
    return (keys, grad * scale, bias * scale, grad_gain * scale)


def by_collectives(hidden_in, segment_ids, key_weight, norm_gain, key_bias, key_cotangent):
    tok_rows = hidden_in.shape[0]
    n_cycle = lax.axis_size("blk")
    n_rep = lax.axis_size("dp")
    positions = positions_of(segment_ids).reshape(tok_rows)
    xf = hidden_in.astype(F32)
    normed = xf * lax.rsqrt(jnp.mean(xf * xf, axis=1, keepdims=True) + 1e-06)
    scaled = (normed * norm_gain[None, :]).astype(BF16)
    cosine, sine = angles_of(positions, HEAD)
    dproj = rotate(key_cotangent.astype(F32), cosine, sine, -1.0).astype(BF16)
    full_weight = lax.all_gather(key_weight, "blk", axis=0, tiled=True)
    projected = jnp.dot(scaled, full_weight, preferred_element_type=F32)
    dscaled = lax.dot_general(
        dproj, full_weight, (((1,), (1,)), ((), ())), preferred_element_type=F32
    )
    projected = projected + key_bias[None, :]
    keys = rotate(projected, cosine, sine, 1.0).astype(BF16)
    cycle_part = lax.psum_scatter(
        lax.dot_general(scaled, dproj, (((0,), (0,)), ((), ())), preferred_element_type=F32),
        "blk",
        scatter_dimension=0,
        tiled=True,
    )
    grad_weight = lax.psum(cycle_part, "dp")
    bias_part = jnp.sum(dproj.astype(F32), axis=0)
    gain_part = jnp.sum(dscaled * normed, axis=0)
    grad_bias, grad_gain = lax.psum((bias_part, gain_part), ("blk", "dp"))
    scale = 1.0 / jnp.sqrt(F32(tok_rows * n_cycle * n_rep))
    return (keys, grad_weight * scale, grad_bias * scale, grad_gain * scale)


def solution(mesh):
    small = mesh.shape["blk"] == 8 and mesh.shape["dp"] == 4
    return jax.shard_map(
        by_permutes if small else by_collectives,
        mesh=mesh,
        in_specs=(
            P(("blk", "dp"), None),
            P(("blk", "dp"), None),
            P("blk", None),
            P(),
            P(),
            P(("blk", "dp"), None),
        ),
        out_specs=(P(("blk", "dp"), None), P("blk", None), P(), P()),
        check_vma=False,
    )
```

```python
import functools

import jax
import jax.numpy as jnp
from jax import lax
from jax.experimental import pallas as pl
from jax.experimental.pallas import tpu as pltpu
from jax.sharding import PartitionSpec as P

KVH = 4
HEAD = 128
KW = 512
F32 = jnp.float32
BF16 = jnp.bfloat16


def positions_of(segs):
    same = segs[:, :, None] == segs[:, None, :]
    idx = jnp.arange(segs.shape[1], dtype=jnp.int32)
    earlier = idx[None, :] < idx[:, None]
    return jnp.sum((same & earlier[None]).astype(jnp.int32), axis=2)


def angles_of(pos, head):
    half = head // 2
    freq = jnp.arange(half, dtype=F32) * (2.0 / head)
    inv = jnp.power(F32(1000000.0), -freq)
    ang = pos.astype(F32)[:, None] * inv[None, :]
    return (jnp.cos(ang)[:, None, :], jnp.sin(ang)[:, None, :])


def rotate(values, cosine, sine, sign):
    rows = values.shape[0]
    heads = values.reshape(rows, KVH, HEAD)
    first = heads[:, :, : HEAD // 2]
    second = heads[:, :, HEAD // 2 :]
    out_a = first * cosine - sign * second * sine
    out_b = second * cosine + sign * first * sine
    return jnp.concatenate([out_a, out_b], axis=2).reshape(rows, KW)


def after(value, *others):
    return lax.optimization_barrier((value, *others))[0]


def call(body, out_shape, name):
    return pl.pallas_call(
        body,
        out_shape=out_shape,
        cost_estimate=pl.CostEstimate(flops=1, bytes_accessed=1, transcendentals=0),
        compiler_params=pltpu.CompilerParams(vmem_limit_bytes=10 * 1024 * 1024),
        name=name,
    )


def scale_body(at_ref, x_ref, gain_ref, *outs):
    wide = x_ref.shape[1]
    part = wide // 8
    half = part // 2
    total = None
    for b in range(8):
        xb = x_ref[:, b * part : (b + 1) * part].astype(F32)
        add = jnp.sum(xb * xb, axis=1, keepdims=True)
        total = add if total is None else total + add
    inv = lax.rsqrt(total * (1.0 / wide) + 1e-06)
    me = at_ref[0]
    mine, sib, rest = outs[:8], outs[8:12], outs[12]
    places = {8 + 3: 0, 8 + 1: 1, 8 + 2: 2, 12 + 3: 3}
    for o in range(8):
        start = pl.multiple_of((me ^ o) * part, part)
        for chunk in range(2):
            cols = pl.ds(start + chunk * half, half)
            xb = x_ref[:, cols].astype(F32)
            done = (xb * inv * gain_ref[:, cols]).astype(BF16)
            at = 4 * chunk + o // 2
            if not o & 1:
                mine[at][...] = done
            elif 8 + at in places:
                sib[places[8 + at]][...] = done
            else:
                at = max(at - 3, 0) * half
                rest[:, at : at + half] = done


def scaled_parts(x, gain, at):
    rows, wide = x.shape
    step = 64
    widths = [wide // 16] * 12 + [wide // 4]
    return pl.pallas_call(
        scale_body,
        grid_spec=pltpu.PrefetchScalarGridSpec(
            num_scalar_prefetch=1,
            grid=(rows // step,),
            in_specs=[
                pl.BlockSpec((step, wide), lambda r, at: (r, 0)),
                pl.BlockSpec((1, wide), lambda r, at: (0, 0)),
            ],
            out_specs=[pl.BlockSpec((step, n), lambda r, at: (r, 0)) for n in widths],
        ),
        out_shape=[jax.ShapeDtypeStruct((rows, n), BF16) for n in widths],
        cost_estimate=pl.CostEstimate(flops=1, bytes_accessed=1, transcendentals=0),
        compiler_params=pltpu.CompilerParams(vmem_limit_bytes=12 * 1024 * 1024),
        name="scale_rows",
    )(at, x, gain[None, :])


def turn(v, cosine, sine):
    return v * cosine + pltpu.roll(v, HEAD // 2, 1) * sine


def turn_body(v_ref, cos_ref, sin_ref, out_ref):
    for h in range(KVH):
        cols = slice(h * HEAD, (h + 1) * HEAD)
        out_ref[:, cols] = turn(v_ref[:, cols].astype(F32), cos_ref[...], sin_ref[...]).astype(BF16)


def keys_body(here, there, bias, cos_ref, sin_ref, out_ref):
    for h in range(KVH):
        cols = slice(h * HEAD, (h + 1) * HEAD)
        v = here[:, cols] + there[:, cols] + bias[:, cols]
        out_ref[:, cols] = turn(v, cos_ref[...], -sin_ref[...]).astype(BF16)


def product(mine, sib, dproj, dproj_sib):
    dims = (((0,), (0,)), ((), ()))
    return lax.dot_general(mine, dproj, dims, preferred_element_type=F32) + lax.dot_general(
        sib, dproj_sib, dims, preferred_element_type=F32
    )


def spread(rows, chip, outs):
    to_x, to_y, keep_y, keep_x = outs
    half = rows.shape[0] // 2
    low = {1: (to_x, 0), 3: (to_x, half), 2: (keep_y, 0)}[chip]
    high = {2: (to_y, 0), 3: (to_y, half), 1: (keep_x, 0)}[chip]
    for (ref, at), part in ((low, rows[:half]), (high, rows[half:])):
        ref[at : at + half] = part.astype(ref.dtype)


def first_grad_body(m1, m2, m3, s1, s2, s3, dproj, dproj_sib, *outs):
    for chip, mine, sib in ((3, m3, s3), (1, m1, s1), (2, m2, s2)):
        spread(product(mine[...], sib[...], dproj[...], dproj_sib[...]), chip, outs)


def second_grad_body(m_a0, m0, m1, m2, m3, s3, rest, dproj, dproj_sib, own_a, own_b, *outs):
    half = m0.shape[1]
    own_a[...] = product(m_a0[...], rest[:, :half], dproj[...], dproj_sib[...])
    for chip, mine in ((3, m3), (1, m1), (2, m2), (0, m0)):
        sib = s3[...] if chip == 3 else rest[:, (chip + 1) * half : (chip + 2) * half]
        rows = product(mine[...], sib, dproj[...], dproj_sib[...])
        if chip:
            spread(rows, chip, outs)
        else:
            own_b[...] = rows


def forward_body(weights_of, *refs):
    places, n_acts, n_init = weights_of
    acts, init, weights, outs = (
        refs[:n_acts],
        refs[n_acts : n_acts + n_init],
        refs[n_acts + n_init : -2],
        refs[-2:],
    )
    for side, out in enumerate(outs):
        total = init[side][...] if n_init else None
        for mine, sib, col, w, row in places:
            half = acts[0].shape[1]
            rows = acts[sib][:, col * half : (col + 1) * half] if side else acts[mine][...]
            add = jnp.dot(
                rows, weights[w][row * half : (row + 1) * half], preferred_element_type=F32
            )
            total = add if total is None else total + add
        out[...] = total


def forward(acts, places, weights, init=()):
    tok, kw = acts[0].shape[0], weights[0].shape[1]
    return call(
        functools.partial(forward_body, (places, len(acts), len(init))),
        [jax.ShapeDtypeStruct((tok, kw), F32)] * 2,
        "forward",
    )(*acts, *init, *weights)


def by_permutes(hidden_in, segment_ids, key_weight, norm_gain, key_bias, key_cotangent):
    tok = hidden_in.shape[0]
    me = lax.axis_index("blk")
    own, kw = key_weight.shape
    half = own // 2
    quarter = own // 4

    def over(bit):
        return lambda v: lax.ppermute(v, "blk", [(i, i ^ bit) for i in range(8)])

    core, px, py = over(1), over(2), over(4)

    def widen(v):
        return v.astype(F32)

    w_x, w_y = px(key_weight), py(key_weight)

    positions = positions_of(segment_ids).reshape(tok)
    lane = jnp.arange(HEAD, dtype=jnp.int32)
    freq = (lane % (HEAD // 2)).astype(F32) * (2.0 / HEAD)
    angle = positions.astype(F32)[:, None] * jnp.power(F32(1000000.0), -freq)[None, :]
    cosine = jnp.cos(angle)
    sine = jnp.sin(angle) * jnp.where(lane < HEAD // 2, 1.0, -1.0)[None, :]
    dproj = call(turn_body, jax.ShapeDtypeStruct((tok, kw), BF16), "turn_back")(
        key_cotangent, cosine, sine
    )
    n = tok // 2
    dproj_sib = jnp.concatenate([core(dproj[:n]), core(dproj[n:])], axis=0)

    parts = scaled_parts(
        after(hidden_in, dproj_sib), norm_gain, me.reshape(1).astype(jnp.int32)
    )
    mine_a, mine_b, (s_a3, s_a1, s_a2, s_b3, rest) = parts[:4], parts[4:8], parts[8:]
    s_a3, s_a1, s_a2 = core(s_a3), core(s_a1), core(s_a2)

    def part_shapes(h):
        shapes = ((2 * h, BF16), (2 * h, BF16), (h, BF16), (h, BF16))
        return [jax.ShapeDtypeStruct((r, kw), t) for r, t in shapes]

    def add_up(part, from_x, from_y):
        _, _, keep_y, keep_x = part
        more_y = (widen(keep_y) + widen(from_x[quarter:])).astype(BF16)
        more_x = (widen(keep_x) + widen(from_y[quarter:])).astype(BF16)
        return more_y, more_x

    def own_rows(mine, first, second):
        low = mine[:quarter] + widen(first[0][:quarter]) + widen(second[0])
        high = mine[quarter:] + widen(first[1][:quarter]) + widen(second[1])
        return low, high

    odd = (lax.axis_index("dp") & 1) == 1

    def over_z(bit):
        return lambda v: lax.ppermute(v, "dp", [(i, i ^ bit) for i in range(4)])

    def in_pair(low, high):
        sent = jnp.where(odd, low, high).astype(BF16)
        return over_z(1)(sent)

    def pair_sum(low, high, into):
        return (jnp.where(odd, high, low) + widen(into)).astype(BF16)

    def total_of(pair, other):
        return (widen(pair) + widen(other)).astype(BF16)

    def both(total, got):
        return widen(jnp.where(odd, got, total)), widen(jnp.where(odd, total, got))

    part_a = call(first_grad_body, part_shapes(quarter), "grad_a")(
        *mine_a[1:], s_a1, s_a2, s_a3, dproj, dproj_sib
    )
    to_a = after((part_a[0], part_a[1]), w_x, w_y)
    in_a = px(to_a[0]), py(to_a[1])
    s_b3, rest = after((s_b3, rest), part_a, w_x, w_y)
    s_b3, rest = core(s_b3), core(rest)
    own_shape = jax.ShapeDtypeStruct((half, kw), F32)
    own_a, own_b, *part_b = call(
        second_grad_body, [own_shape, own_shape, *part_shapes(quarter)], "grad_b"
    )(mine_a[0], *mine_b, s_b3, rest, dproj, dproj_sib)

    acts = (*mine_a[:3], *mine_b[:3], s_a1, s_a2, rest)
    places = (
        (0, 8, 0, 0, 0),
        (3, 8, 1, 0, 1),
        (1, 6, 0, 1, 0),
        (4, 8, 2, 1, 1),
        (2, 7, 0, 2, 0),
        (5, 8, 3, 2, 1),
    )
    here = forward(acts, places, (after(key_weight, part_b), w_x, w_y))

    in_a = after(in_a, here)
    to_b = after((part_b[0], part_b[1]), in_a)
    more = add_up(part_a, *in_a)
    two_a = py(more[0]), px(more[1])
    in_b = px(to_b[0]), py(to_b[1])
    local_a = own_rows(own_a, in_a, two_a)
    pair_a = pair_sum(*local_a, in_pair(*local_a))

    in_b = after(in_b, two_a)
    more = after(add_up(part_b, *in_b), pair_a)
    two_b = py(more[0]), px(more[1])
    later = after((w_y[:half], w_x[half:]), pair_a)
    wd_low, wd_high = px(later[0]), py(later[1])
    total_a = total_of(pair_a, over_z(2)(pair_a))
    got_a = over_z(1)(total_a)
    local_b = after(own_rows(own_b, in_b, two_b), total_a)
    into_b, wd_low, wd_high = after((in_pair(*local_b), wd_low, wd_high))
    pair_b = pair_sum(*local_b, into_b)

    acts = after((mine_a[3], mine_b[3], s_a3, s_b3), pair_b)
    here, there = forward(acts, ((0, 2, 0, 0, 0), (1, 3, 0, 1, 0)), (wd_low, wd_high), here)
    keys = call(keys_body, jax.ShapeDtypeStruct((tok, kw), BF16), "keys")(
        here, core(there), key_bias[None, :], cosine, sine
    )

    local = after((*local_a, *local_b), pair_b)
    my_gain = lax.dynamic_slice(norm_gain, (me * own,), (own,))
    gain_rows = jnp.concatenate(
        [
            jnp.sum(v * widen(key_weight[n * quarter : (n + 1) * quarter]), axis=1)
            for n, v in enumerate(local)
        ]
    )
    bias = jnp.sum(widen(dproj), axis=0) + jnp.sum(widen(dproj_sib), axis=0)
    n_own = own // HEAD
    small = jnp.concatenate([gain_rows / my_gain, bias]).reshape(-1, HEAD)
    for bit in (1, 2):
        small = small + over_z(bit)(small)
    gains, bias = small[:n_own], small[n_own:]
    scale = 1.0 / jnp.sqrt(F32(tok * 32))
    for bit in (1, 2, 4):
        got = over(bit)(jnp.concatenate([gains, bias], axis=0))
        if bit == 1:
            got, other_b, got_a = after((got, over_z(2)(pair_b), got_a))
            total_b = total_of(pair_b, other_b)
            got_b = over_z(1)(total_b)
        size = gains.shape[0]
        theirs = got[:size]
        first = (me & bit) == 0
        gains = jnp.concatenate(
            [jnp.where(first, gains, theirs), jnp.where(first, theirs, gains)], axis=0
        )
        if bit > 1:
            bias = bias + got[size:]
    got_b, keys, gains, bias = after((got_b, keys, gains, bias))
    grad = jnp.concatenate([*both(total_a, got_a), *both(total_b, got_b)], axis=0)
    return (keys, grad * scale, bias.reshape(-1) * scale, gains.reshape(-1) * scale)


def by_collectives(hidden_in, segment_ids, key_weight, norm_gain, key_bias, key_cotangent):
    tok_rows = hidden_in.shape[0]
    n_cycle = lax.axis_size("blk")
    n_rep = lax.axis_size("dp")
    positions = positions_of(segment_ids).reshape(tok_rows)
    xf = hidden_in.astype(F32)
    normed = xf * lax.rsqrt(jnp.mean(xf * xf, axis=1, keepdims=True) + 1e-06)
    scaled = (normed * norm_gain[None, :]).astype(BF16)
    cosine, sine = angles_of(positions, HEAD)
    dproj = rotate(key_cotangent.astype(F32), cosine, sine, -1.0).astype(BF16)
    full_weight = lax.all_gather(key_weight, "blk", axis=0, tiled=True)
    projected = jnp.dot(scaled, full_weight, preferred_element_type=F32)
    dscaled = lax.dot_general(
        dproj, full_weight, (((1,), (1,)), ((), ())), preferred_element_type=F32
    )
    projected = projected + key_bias[None, :]
    keys = rotate(projected, cosine, sine, 1.0).astype(BF16)
    cycle_part = lax.psum_scatter(
        lax.dot_general(scaled, dproj, (((0,), (0,)), ((), ())), preferred_element_type=F32),
        "blk",
        scatter_dimension=0,
        tiled=True,
    )
    grad_weight = lax.psum(cycle_part, "dp")
    bias_part = jnp.sum(dproj.astype(F32), axis=0)
    gain_part = jnp.sum(dscaled * normed, axis=0)
    grad_bias, grad_gain = lax.psum((bias_part, gain_part), ("blk", "dp"))
    scale = 1.0 / jnp.sqrt(F32(tok_rows * n_cycle * n_rep))
    return (keys, grad_weight * scale, grad_bias * scale, grad_gain * scale)


def solution(mesh):
    small = mesh.shape["blk"] == 8 and mesh.shape["dp"] == 4
    return jax.shard_map(
        by_permutes if small else by_collectives,
        mesh=mesh,
        in_specs=(
            P(("blk", "dp"), None),
            P(("blk", "dp"), None),
            P("blk", None),
            P(),
            P(),
            P(("blk", "dp"), None),
        ),
        out_specs=(P(("blk", "dp"), None), P("blk", None), P(), P()),
        check_vma=False,
    )
```

```python
import functools

import jax
import jax.numpy as jnp
import numpy as np
from jax import lax
from jax.experimental import pallas as pl
from jax.experimental.pallas import tpu as pltpu
from jax.sharding import PartitionSpec as P

KVH = 4
HEAD = 128
KW = 512
F32 = jnp.float32
BF16 = jnp.bfloat16


def positions_of(segs):
    same = segs[:, :, None] == segs[:, None, :]
    idx = jnp.arange(segs.shape[1], dtype=jnp.int32)
    earlier = idx[None, :] < idx[:, None]
    return jnp.sum((same & earlier[None]).astype(jnp.int32), axis=2)


def angles_of(pos, head):
    half = head // 2
    freq = jnp.arange(half, dtype=F32) * (2.0 / head)
    inv = jnp.power(F32(1000000.0), -freq)
    ang = pos.astype(F32)[:, None] * inv[None, :]
    return (jnp.cos(ang)[:, None, :], jnp.sin(ang)[:, None, :])


def rotate(values, cosine, sine, sign):
    rows = values.shape[0]
    heads = values.reshape(rows, KVH, HEAD)
    first = heads[:, :, : HEAD // 2]
    second = heads[:, :, HEAD // 2 :]
    out_a = first * cosine - sign * second * sine
    out_b = second * cosine + sign * first * sine
    return jnp.concatenate([out_a, out_b], axis=2).reshape(rows, KW)


def after(value, *others):
    return lax.optimization_barrier((value, *others))[0]


def call(body, out_shape, name):
    return pl.pallas_call(
        body,
        out_shape=out_shape,
        cost_estimate=pl.CostEstimate(flops=1, bytes_accessed=1, transcendentals=0),
        compiler_params=pltpu.CompilerParams(vmem_limit_bytes=10 * 1024 * 1024),
        name=name,
    )


def turn(v, cosine, sine):
    return v * cosine + pltpu.roll(v, HEAD // 2, 1) * sine


def prepare_body(per_batch, at_ref, x_ref, gain_ref, seg_ref, inv_ref, cot_ref, *outs):
    step, wide = x_ref.shape
    part = wide // 8
    half = part // 2
    total = None
    for b in range(8):
        xb = x_ref[:, b * part : (b + 1) * part].astype(F32)
        add = jnp.sum(xb * xb, axis=1, keepdims=True)
        total = add if total is None else total + add
    inv = lax.rsqrt(total * (1.0 / wide) + 1e-06)
    me = at_ref[0]
    mine, sib, rest = outs[:8], outs[8:12], outs[12]
    cos_ref, sin_ref, dproj_ref = outs[13:]
    places = {3: 0, 1: 1, 2: 2, 7: 3}
    for o in range(8):
        start = pl.multiple_of((me ^ o) * part, part)
        for chunk in range(2):
            cols = pl.ds(start + chunk * half, half)
            xb = x_ref[:, cols].astype(F32)
            done = (xb * inv * gain_ref[:, cols]).astype(BF16)
            at = 4 * chunk + o // 2
            if not o & 1:
                mine[at][...] = done
            elif at in places:
                sib[places[at]][...] = done
            else:
                at = max(at - 3, 0) * half
                rest[:, at : at + half] = done

    r = pl.program_id(0)
    seq = seg_ref.shape[1]
    segs = seg_ref[pl.ds(r // per_batch, 1), :]
    row = lax.broadcasted_iota(jnp.int32, (step, seq), 0) + r % per_batch * step
    col = lax.broadcasted_iota(jnp.int32, (step, seq), 1)
    own = jnp.sum(jnp.where(row == col, segs, 0), axis=1, keepdims=True)
    position = jnp.sum(
        jnp.where((own == segs) & (col < row), 1, 0), axis=1, keepdims=True
    )
    angle = position.astype(F32) * inv_ref[...]
    cosine, sine = jnp.cos(angle), jnp.sin(angle)
    second = lax.broadcasted_iota(jnp.int32, sine.shape, 1) >= HEAD // 2
    sine = jnp.where(second, -sine, sine)
    cos_ref[...] = cosine
    sin_ref[...] = sine
    for h in range(KVH):
        cols = slice(h * HEAD, (h + 1) * HEAD)
        dproj_ref[:, cols] = turn(cot_ref[:, cols].astype(F32), cosine, sine).astype(BF16)


def prepared(x, gain, segs, cotangent, at):
    rows, wide = x.shape
    step = 64
    half = wide // 16
    outs = [(half, BF16)] * 12 + [(4 * half, BF16), (HEAD, F32), (HEAD, F32), (KW, BF16)]
    freq = np.arange(HEAD) % (HEAD // 2) * (2.0 / HEAD)
    inv = jnp.asarray(np.power(1000000.0, -freq)[None, :], F32)

    def whole(v):
        return pl.BlockSpec(v.shape, lambda r, at: (0, 0))

    def some(n):
        return pl.BlockSpec((step, n), lambda r, at: (r, 0))

    gain = gain[None, :]
    return pl.pallas_call(
        functools.partial(prepare_body, segs.shape[1] // step),
        grid_spec=pltpu.PrefetchScalarGridSpec(
            num_scalar_prefetch=1,
            grid=(rows // step,),
            in_specs=[some(wide), whole(gain), whole(segs), whole(inv), some(KW)],
            out_specs=[some(n) for n, _ in outs],
        ),
        out_shape=[jax.ShapeDtypeStruct((rows, n), t) for n, t in outs],
        cost_estimate=pl.CostEstimate(flops=1, bytes_accessed=1, transcendentals=0),
        compiler_params=pltpu.CompilerParams(vmem_limit_bytes=14 * 1024 * 1024),
        name="prepare",
    )(at, x, gain, segs, inv, cotangent)


def keys_body(here, there, bias, cos_ref, sin_ref, out_ref):
    for h in range(KVH):
        cols = slice(h * HEAD, (h + 1) * HEAD)
        v = here[:, cols] + there[:, cols] + bias[:, cols]
        out_ref[:, cols] = turn(v, cos_ref[...], -sin_ref[...]).astype(BF16)


def product(mine, sib, dproj, dproj_sib):
    dims = (((0,), (0,)), ((), ()))
    return lax.dot_general(mine, dproj, dims, preferred_element_type=F32) + lax.dot_general(
        sib, dproj_sib, dims, preferred_element_type=F32
    )


def spread(rows, chip, outs):
    to_x, to_y, keep_y, keep_x = outs
    half = rows.shape[0] // 2
    low = {1: (to_x, 0), 3: (to_x, half), 2: (keep_y, 0)}[chip]
    high = {2: (to_y, 0), 3: (to_y, half), 1: (keep_x, 0)}[chip]
    for (ref, at), part in ((low, rows[:half]), (high, rows[half:])):
        ref[at : at + half] = part.astype(ref.dtype)


def first_grad_body(m1, m2, m3, s1, s2, s3, dproj, upper, lower, *outs):
    dproj_sib = jnp.concatenate([upper[...], lower[...]], axis=0)
    for chip, mine, sib in ((3, m3, s3), (1, m1, s1), (2, m2, s2)):
        spread(product(mine[...], sib[...], dproj[...], dproj_sib), chip, outs)


def second_grad_body(m_a0, m0, m1, m2, m3, s3, rest, dproj, upper, lower, own_a, own_b, *outs):
    dproj_sib = jnp.concatenate([upper[...], lower[...]], axis=0)
    half = m0.shape[1]
    own_a[...] = product(m_a0[...], rest[:, :half], dproj[...], dproj_sib)
    for chip, mine in ((3, m3), (1, m1), (2, m2), (0, m0)):
        sib = s3[...] if chip == 3 else rest[:, (chip + 1) * half : (chip + 2) * half]
        rows = product(mine[...], sib, dproj[...], dproj_sib)
        if chip:
            spread(rows, chip, outs)
        else:
            own_b[...] = rows


def forward_body(weights_of, *refs):
    places, n_acts, n_init = weights_of
    acts, init, weights, outs = (
        refs[:n_acts],
        refs[n_acts : n_acts + n_init],
        refs[n_acts + n_init : -2],
        refs[-2:],
    )
    for side, out in enumerate(outs):
        total = init[side][...] if n_init else None
        for mine, sib, col, w, row in places:
            half = acts[0].shape[1]
            rows = acts[sib][:, col * half : (col + 1) * half] if side else acts[mine][...]
            add = jnp.dot(
                rows, weights[w][row * half : (row + 1) * half], preferred_element_type=F32
            )
            total = add if total is None else total + add
        out[...] = total


def forward(acts, places, weights, init=()):
    tok, kw = acts[0].shape[0], weights[0].shape[1]
    return call(
        functools.partial(forward_body, (places, len(acts), len(init))),
        [jax.ShapeDtypeStruct((tok, kw), F32)] * 2,
        "forward",
    )(*acts, *init, *weights)


def by_permutes(hidden_in, segment_ids, key_weight, norm_gain, key_bias, key_cotangent):
    tok = hidden_in.shape[0]
    me = lax.axis_index("blk")
    own, kw = key_weight.shape
    half = own // 2
    quarter = own // 4

    def over(bit):
        return lambda v: lax.ppermute(v, "blk", [(i, i ^ bit) for i in range(8)])

    core, px, py = over(1), over(2), over(4)

    def widen(v):
        return v.astype(F32)

    odd = (lax.axis_index("dp") & 1) == 1
    firsts = [(me & bit) == 0 for bit in (1, 2, 4)]
    my_gain = lax.dynamic_slice(norm_gain, (me * own,), (own,))
    at = me.reshape(1).astype(jnp.int32)
    odd, firsts, my_gain, at, key_weight, hidden_in, key_cotangent, segment_ids = after(
        (odd, firsts, my_gain, at, key_weight, hidden_in, key_cotangent, segment_ids)
    )
    w_x, w_y = px(key_weight), py(key_weight)

    parts = prepared(hidden_in, norm_gain, segment_ids, key_cotangent, at)
    mine_a, mine_b, (s_a3, s_a1, s_a2, s_b3, rest) = parts[:4], parts[4:8], parts[8:13]
    cosine, sine, dproj = parts[13:]
    n = tok // 2
    dproj_sib = core(dproj[:n]), core(dproj[n:])
    s_a3, s_a1, s_a2 = core(s_a3), core(s_a1), core(s_a2)

    def part_shapes(h):
        shapes = ((2 * h, BF16), (2 * h, BF16), (h, BF16), (h, BF16))
        return [jax.ShapeDtypeStruct((r, kw), t) for r, t in shapes]

    def add_up(part, from_x, from_y):
        _, _, keep_y, keep_x = part
        more_y = (widen(keep_y) + widen(from_x[quarter:])).astype(BF16)
        more_x = (widen(keep_x) + widen(from_y[quarter:])).astype(BF16)
        return more_y, more_x

    def own_rows(mine, first, second):
        low = mine[:quarter] + widen(first[0][:quarter]) + widen(second[0])
        high = mine[quarter:] + widen(first[1][:quarter]) + widen(second[1])
        return low, high

    def over_z(bit):
        return lambda v: lax.ppermute(v, "dp", [(i, i ^ bit) for i in range(4)])

    def in_pair(low, high):
        sent = jnp.where(odd, low, high).astype(BF16)
        return over_z(1)(sent)

    def pair_sum(low, high, into):
        return (jnp.where(odd, high, low) + widen(into)).astype(BF16)

    def total_of(pair, other):
        return (widen(pair) + widen(other)).astype(BF16)

    def both(total, got):
        return widen(jnp.where(odd, got, total)), widen(jnp.where(odd, total, got))

    part_a = call(first_grad_body, part_shapes(quarter), "grad_a")(
        *mine_a[1:], s_a1, s_a2, s_a3, dproj, *dproj_sib
    )
    to_a = after((part_a[0], part_a[1]), w_x, w_y)
    in_a = px(to_a[0]), py(to_a[1])
    s_b3, rest = after((s_b3, rest), part_a, w_x, w_y)
    s_b3, rest = core(s_b3), core(rest)
    own_shape = jax.ShapeDtypeStruct((half, kw), F32)
    own_a, own_b, *part_b = call(
        second_grad_body, [own_shape, own_shape, *part_shapes(quarter)], "grad_b"
    )(mine_a[0], *mine_b, s_b3, rest, dproj, *dproj_sib)

    acts = (*mine_a[:3], *mine_b[:3], s_a1, s_a2, rest)
    places = (
        (0, 8, 0, 0, 0),
        (3, 8, 1, 0, 1),
        (1, 6, 0, 1, 0),
        (4, 8, 2, 1, 1),
        (2, 7, 0, 2, 0),
        (5, 8, 3, 2, 1),
    )
    here = forward(acts, places, (after(key_weight, part_b), w_x, w_y))

    in_a = after(in_a, here)
    to_b = after((part_b[0], part_b[1]), in_a)
    more = add_up(part_a, *in_a)
    two_a = py(more[0]), px(more[1])
    in_b = px(to_b[0]), py(to_b[1])
    local_a = own_rows(own_a, in_a, two_a)
    pair_a = pair_sum(*local_a, in_pair(*local_a))

    in_b = after(in_b, two_a)
    more = after(add_up(part_b, *in_b), pair_a)
    two_b = py(more[0]), px(more[1])
    later = after((w_y[:half], w_x[half:]), two_b)
    wd_low, wd_high = px(later[0]), py(later[1])
    total_a = total_of(pair_a, over_z(2)(pair_a))
    got_a = over_z(1)(total_a)
    local_b = after(own_rows(own_b, in_b, two_b), total_a)
    into_b = in_pair(*local_b)

    gain_rows = jnp.concatenate(
        [
            jnp.sum(v * widen(key_weight[n * quarter : (n + 1) * quarter]), axis=1)
            for n, v in enumerate((*local_a, *local_b))
        ]
    )
    bias = sum(jnp.sum(widen(v), axis=0) for v in (dproj, *dproj_sib))
    n_own = own // HEAD
    small = jnp.concatenate([gain_rows / my_gain, bias]).reshape(-1, HEAD)
    small = small + over_z(1)(small)
    into_b, small = after((into_b, small))
    pair_b = pair_sum(*local_b, into_b)
    small = small + over_z(2)(small)
    other_b, got_a, small = after((over_z(2)(pair_b), got_a, small))
    total_b = total_of(pair_b, other_b)
    got_b = over_z(1)(total_b)

    acts = after((mine_a[3], mine_b[3], s_a3, s_b3), pair_b)
    here, there = forward(acts, ((0, 2, 0, 0, 0), (1, 3, 0, 1, 0)), (wd_low, wd_high), here)
    keys = call(keys_body, jax.ShapeDtypeStruct((tok, kw), BF16), "keys")(
        here, core(there), key_bias[None, :], cosine, sine
    )

    gains, bias = small[:n_own], small[n_own:]
    scale = 1.0 / jnp.sqrt(F32(tok * 32))
    for bit, first in zip((1, 2, 4), firsts, strict=True):
        got = over(bit)(jnp.concatenate([gains, bias], axis=0))
        size = gains.shape[0]
        theirs = got[:size]
        gains = jnp.concatenate(
            [jnp.where(first, gains, theirs), jnp.where(first, theirs, gains)], axis=0
        )
        if bit > 1:
            bias = bias + got[size:]
    got_b, keys, gains, bias = after((got_b, keys, gains, bias))
    grad = jnp.concatenate([*both(total_a, got_a), *both(total_b, got_b)], axis=0)
    return (keys, grad * scale, bias.reshape(-1) * scale, gains.reshape(-1) * scale)


def by_collectives(hidden_in, segment_ids, key_weight, norm_gain, key_bias, key_cotangent):
    tok_rows = hidden_in.shape[0]
    n_cycle = lax.axis_size("blk")
    n_rep = lax.axis_size("dp")
    positions = positions_of(segment_ids).reshape(tok_rows)
    xf = hidden_in.astype(F32)
    normed = xf * lax.rsqrt(jnp.mean(xf * xf, axis=1, keepdims=True) + 1e-06)
    scaled = (normed * norm_gain[None, :]).astype(BF16)
    cosine, sine = angles_of(positions, HEAD)
    dproj = rotate(key_cotangent.astype(F32), cosine, sine, -1.0).astype(BF16)
    full_weight = lax.all_gather(key_weight, "blk", axis=0, tiled=True)
    projected = jnp.dot(scaled, full_weight, preferred_element_type=F32)
    dscaled = lax.dot_general(
        dproj, full_weight, (((1,), (1,)), ((), ())), preferred_element_type=F32
    )
    projected = projected + key_bias[None, :]
    keys = rotate(projected, cosine, sine, 1.0).astype(BF16)
    cycle_part = lax.psum_scatter(
        lax.dot_general(scaled, dproj, (((0,), (0,)), ((), ())), preferred_element_type=F32),
        "blk",
        scatter_dimension=0,
        tiled=True,
    )
    grad_weight = lax.psum(cycle_part, "dp")
    bias_part = jnp.sum(dproj.astype(F32), axis=0)
    gain_part = jnp.sum(dscaled * normed, axis=0)
    grad_bias, grad_gain = lax.psum((bias_part, gain_part), ("blk", "dp"))
    scale = 1.0 / jnp.sqrt(F32(tok_rows * n_cycle * n_rep))
    return (keys, grad_weight * scale, grad_bias * scale, grad_gain * scale)


def solution(mesh):
    small = mesh.shape["blk"] == 8 and mesh.shape["dp"] == 4
    return jax.shard_map(
        by_permutes if small else by_collectives,
        mesh=mesh,
        in_specs=(
            P(("blk", "dp"), None),
            P(("blk", "dp"), None),
            P("blk", None),
            P(),
            P(),
            P(("blk", "dp"), None),
        ),
        out_specs=(P(("blk", "dp"), None), P("blk", None), P(), P()),
        check_vma=False,
    )
```

```python
import functools
import math

import jax
import jax.numpy as jnp
from jax import lax
from jax.experimental import pallas as pl
from jax.experimental.pallas import tpu as pltpu
from jax.sharding import PartitionSpec as P

KVH = 4
HEAD = 128
KW = 512
F32 = jnp.float32
BF16 = jnp.bfloat16


def positions_of(segs):
    same = segs[:, :, None] == segs[:, None, :]
    idx = jnp.arange(segs.shape[1], dtype=jnp.int32)
    earlier = idx[None, :] < idx[:, None]
    return jnp.sum((same & earlier[None]).astype(jnp.int32), axis=2)


def angles_of(pos, head):
    half = head // 2
    freq = jnp.arange(half, dtype=F32) * (2.0 / head)
    inv = jnp.power(F32(1000000.0), -freq)
    ang = pos.astype(F32)[:, None] * inv[None, :]
    return (jnp.cos(ang)[:, None, :], jnp.sin(ang)[:, None, :])


def rotate(values, cosine, sine, sign):
    rows = values.shape[0]
    heads = values.reshape(rows, KVH, HEAD)
    first = heads[:, :, : HEAD // 2]
    second = heads[:, :, HEAD // 2 :]
    out_a = first * cosine - sign * second * sine
    out_b = second * cosine + sign * first * sine
    return jnp.concatenate([out_a, out_b], axis=2).reshape(rows, KW)


def after(value, *others):
    return lax.optimization_barrier((value, *others))[0]


def call(body, out_shape, name):
    return pl.pallas_call(
        body,
        out_shape=out_shape,
        cost_estimate=pl.CostEstimate(flops=1, bytes_accessed=1, transcendentals=0),
        compiler_params=pltpu.CompilerParams(vmem_limit_bytes=10 * 1024 * 1024),
        name=name,
    )


def turn(v, cosine, sine):
    return v * cosine + pltpu.roll(v, HEAD // 2, 1) * sine


def prepare_body(per_batch, at_ref, x_ref, gain_ref, seg_ref, cot_ref, *outs):
    step, wide = x_ref.shape
    part = wide // 8
    half = part // 2
    total = None
    for b in range(8):
        xb = x_ref[:, b * part : (b + 1) * part].astype(F32)
        add = jnp.sum(xb * xb, axis=1, keepdims=True)
        total = add if total is None else total + add
    inv = lax.rsqrt(total * (1.0 / wide) + 1e-06)
    me = at_ref[0]
    mine, sib, rest = outs[:8], outs[8:12], outs[12]
    cos_ref, sin_ref, dproj_ref, own_gain_ref = outs[13:]
    own_gain_ref[...] = gain_ref[:, pl.ds(pl.multiple_of(me * part, part), part)]
    places = {3: 0, 1: 1, 2: 2, 7: 3}
    for o in range(8):
        start = pl.multiple_of((me ^ o) * part, part)
        for chunk in range(2):
            cols = pl.ds(start + chunk * half, half)
            xb = x_ref[:, cols].astype(F32)
            done = (xb * inv * gain_ref[:, cols]).astype(BF16)
            at = 4 * chunk + o // 2
            if not o & 1:
                mine[at][...] = done
            elif at in places:
                sib[places[at]][...] = done
            else:
                at = max(at - 3, 0) * half
                rest[:, at : at + half] = done

    r = pl.program_id(0)
    seq = seg_ref.shape[1]
    segs = seg_ref[pl.ds(r // per_batch, 1), :]
    row = lax.broadcasted_iota(jnp.int32, (step, seq), 0) + r % per_batch * step
    col = lax.broadcasted_iota(jnp.int32, (step, seq), 1)
    own = jnp.sum(jnp.where(row == col, segs, 0), axis=1, keepdims=True)
    position = jnp.sum(
        jnp.where((own == segs) & (col < row), 1, 0), axis=1, keepdims=True
    )
    lane = lax.broadcasted_iota(jnp.int32, (1, HEAD), 1)
    second = lane >= HEAD // 2
    freq = (lane % (HEAD // 2)).astype(F32)
    angle = position.astype(F32) * jnp.exp(freq * (-2.0 * math.log(1000000.0) / HEAD))
    pair = jnp.cos(angle - jnp.where(second, math.pi / 2, 0.0).astype(F32))
    swapped = pltpu.roll(pair, HEAD // 2, 1)
    cosine = jnp.where(second, swapped, pair)
    sine = jnp.where(second, -pair, swapped)
    cos_ref[...] = cosine
    sin_ref[...] = sine
    for h in range(KVH):
        cols = slice(h * HEAD, (h + 1) * HEAD)
        dproj_ref[:, cols] = turn(cot_ref[:, cols].astype(F32), cosine, sine).astype(BF16)


def prepared(x, gain, segs, cotangent, at):
    rows, wide = x.shape
    step = 64
    half = wide // 16
    outs = [(half, BF16)] * 12 + [(4 * half, BF16), (HEAD, F32), (HEAD, F32), (KW, BF16)]
    def whole(v):
        return pl.BlockSpec(v.shape, lambda r, at: (0, 0))

    def some(n):
        return pl.BlockSpec((step, n), lambda r, at: (r, 0))

    gain, segs, cotangent = (
        pltpu.with_memory_space_constraint(v, pltpu.HBM) for v in (gain[None, :], segs, cotangent)
    )
    return pl.pallas_call(
        functools.partial(prepare_body, segs.shape[1] // step),
        grid_spec=pltpu.PrefetchScalarGridSpec(
            num_scalar_prefetch=1,
            grid=(rows // step,),
            in_specs=[some(wide), whole(gain), whole(segs), some(KW)],
            out_specs=[
                *(some(n) for n, _ in outs),
                pl.BlockSpec((1, 2 * half), lambda r, at: (0, 0)),
            ],
        ),
        out_shape=[
            *(jax.ShapeDtypeStruct((rows, n), t) for n, t in outs),
            jax.ShapeDtypeStruct((1, 2 * half), F32),
        ],
        cost_estimate=pl.CostEstimate(flops=1, bytes_accessed=1, transcendentals=0),
        compiler_params=pltpu.CompilerParams(vmem_limit_bytes=14 * 1024 * 1024),
        name="prepare",
    )(at, x, gain, segs, cotangent)


def keys_body(here, upper, lower, bias, cos_ref, sin_ref, out_ref):
    for h in range(KVH):
        cols = slice(h * HEAD, (h + 1) * HEAD)
        there = jnp.concatenate([upper[:, cols], lower[:, cols]], axis=0).astype(F32)
        v = here[:, cols] + there + bias[:, cols]
        out_ref[:, cols] = turn(v, cos_ref[...], -sin_ref[...]).astype(BF16)


def product(mine, sib, dproj, dproj_sib):
    dims = (((0,), (0,)), ((), ()))
    return lax.dot_general(mine, dproj, dims, preferred_element_type=F32) + lax.dot_general(
        sib, dproj_sib, dims, preferred_element_type=F32
    )


def spread(rows, chip, outs):
    to_x, to_y, keep_y, keep_x = outs
    half = rows.shape[0] // 2
    low = {1: (to_x, 0), 3: (to_x, half), 2: (keep_y, 0)}[chip]
    high = {2: (to_y, 0), 3: (to_y, half), 1: (keep_x, 0)}[chip]
    for (ref, at), part in ((low, rows[:half]), (high, rows[half:])):
        ref[at : at + half] = part.astype(ref.dtype)


def first_grad_body(m1, m2, m3, s1, s2, s3, dproj, upper, lower, *outs):
    dproj_sib = jnp.concatenate([upper[...], lower[...]], axis=0)
    for chip, mine, sib in ((3, m3, s3), (1, m1, s1), (2, m2, s2)):
        spread(product(mine[...], sib[...], dproj[...], dproj_sib), chip, outs)


def second_grad_body(m_a0, m0, m1, m2, m3, s3, rest, dproj, upper, lower, own_a, own_b, *outs):
    dproj_sib = jnp.concatenate([upper[...], lower[...]], axis=0)
    half = m0.shape[1]
    own_a[...] = product(m_a0[...], rest[:, :half], dproj[...], dproj_sib)
    for chip, mine in ((3, m3), (1, m1), (2, m2), (0, m0)):
        sib = s3[...] if chip == 3 else rest[:, (chip + 1) * half : (chip + 2) * half]
        rows = product(mine[...], sib, dproj[...], dproj_sib)
        if chip:
            spread(rows, chip, outs)
        else:
            own_b[...] = rows


def forward_body(places, n_acts, n_init, *refs):
    acts, init, refs = refs[:n_acts], refs[n_acts : n_acts + n_init], refs[n_acts + n_init :]
    half = acts[0].shape[1]
    n_outs = 3 if n_init else 2
    weights, outs = refs[:-n_outs], refs[-n_outs:]
    totals = [v[...] for v in init] if n_init else [None, None]
    for side in (1, 0):
        total = totals[side]
        for mine, sib, col, pieces in places:
            w = jnp.concatenate([weights[n][at : at + rows] for n, at, rows in pieces], axis=0)
            rows = acts[sib][:, col * half : (col + 1) * half] if side else acts[mine][...]
            add = jnp.dot(rows, w, preferred_element_type=F32)
            total = add if total is None else total + add
        if side and n_init:
            n = outs[1].shape[0]
            outs[1][...] = total[:n].astype(BF16)
            outs[2][...] = total[n:].astype(BF16)
        else:
            outs[side][...] = total


def forward(acts, places, weights, init=()):
    tok, kw = acts[0].shape[0], weights[0].shape[1]
    shape = jax.ShapeDtypeStruct((tok, kw), F32)
    part = jax.ShapeDtypeStruct((tok // 2, kw), BF16)
    return call(
        functools.partial(forward_body, places, len(acts), len(init)),
        [shape, part, part] if init else [shape, shape],
        "forward",
    )(*acts, *init, *weights)


def by_permutes(hidden_in, segment_ids, key_weight, norm_gain, key_bias, key_cotangent):
    tok = hidden_in.shape[0]
    me = lax.axis_index("blk")
    own, kw = key_weight.shape
    half = own // 2
    quarter = own // 4

    def over(bit):
        return lambda v: lax.ppermute(v, "blk", [(i, i ^ bit) for i in range(8)])

    core, px, py = over(1), over(2), over(4)

    def widen(v):
        return v.astype(F32)

    odd = (lax.axis_index("dp") & 1) == 1
    firsts = [(me & bit) == 0 for bit in (1, 2, 4)]
    at = me.reshape(1).astype(jnp.int32)
    odd, firsts, at, key_weight, hidden_in, key_cotangent, segment_ids = after(
        (odd, firsts, at, key_weight, hidden_in, key_cotangent, segment_ids)
    )
    early = half + own * 5 // 16
    late = own - early
    w_x, w_y = px(key_weight[late:]), py(key_weight[:early])

    parts = prepared(hidden_in, norm_gain, segment_ids, key_cotangent, at)
    mine_a, mine_b, (s_a3, s_a1, s_a2, s_b3, rest) = parts[:4], parts[4:8], parts[8:13]
    cosine, sine, dproj, my_gain = parts[13:]
    my_gain = my_gain.reshape(own)
    n = tok // 2
    dproj_sib = core(dproj[:n]), core(dproj[n:])
    s_a3, s_a1, s_a2 = core(s_a3), core(s_a1), core(s_a2)

    def part_shapes(h):
        shapes = ((2 * h, BF16), (2 * h, BF16), (h, BF16), (h, BF16))
        return [jax.ShapeDtypeStruct((r, kw), t) for r, t in shapes]

    def add_up(part, from_x, from_y):
        _, _, keep_y, keep_x = part
        more_y = (widen(keep_y) + widen(from_x[quarter:])).astype(BF16)
        more_x = (widen(keep_x) + widen(from_y[quarter:])).astype(BF16)
        return more_y, more_x

    def own_rows(mine, first, second):
        low = mine[:quarter] + widen(first[0][:quarter]) + widen(second[0])
        high = mine[quarter:] + widen(first[1][:quarter]) + widen(second[1])
        return low, high

    def over_z(bit):
        return lambda v: lax.ppermute(v, "dp", [(i, i ^ bit) for i in range(4)])

    def in_pair(low, high):
        sent = jnp.where(odd, low, high).astype(BF16)
        return over_z(1)(sent)

    def pair_sum(low, high, into):
        return (jnp.where(odd, high, low) + widen(into)).astype(BF16)

    def total_of(pair, other):
        return (widen(pair) + widen(other)).astype(BF16)

    def both(total, got):
        return widen(jnp.where(odd, got, total)), widen(jnp.where(odd, total, got))

    part_a = call(first_grad_body, part_shapes(quarter), "grad_a")(
        *mine_a[1:], s_a1, s_a2, s_a3, dproj, *dproj_sib
    )
    to_a = after((part_a[0], part_a[1]), w_x, w_y)
    in_a = px(to_a[0]), py(to_a[1])
    s_b3, rest = after((s_b3, rest), part_a, w_x, w_y)
    s_b3, rest = core(s_b3), core(rest)
    own_shape = jax.ShapeDtypeStruct((half, kw), F32)
    own_a, own_b, *part_b = call(
        second_grad_body, [own_shape, own_shape, *part_shapes(quarter)], "grad_b"
    )(mine_a[0], *mine_b, s_b3, rest, dproj, *dproj_sib)

    acts = (mine_a[0], mine_b[0], mine_a[2], mine_b[1], s_a2, rest)
    places = (
        (0, 5, 0, ((0, 0, half),)),
        (1, 5, 1, ((0, half, half),)),
        (2, 4, 0, ((1, 0, half),)),
        (3, 5, 2, ((2, early - half, half),)),
    )
    here = forward(acts, places, (after(key_weight, part_b), w_y, w_x))

    in_a = after(in_a, here)
    to_b = after((part_b[0], part_b[1]), in_a)
    more = add_up(part_a, *in_a)
    two_a = py(more[0]), px(more[1])
    in_b = px(to_b[0]), py(to_b[1])
    local_a = own_rows(own_a, in_a, two_a)
    pair_a = pair_sum(*local_a, in_pair(*local_a))

    in_b = after(in_b, two_a)
    more = after(add_up(part_b, *in_b), pair_a)
    two_b = py(more[0]), px(more[1])
    w_y, w_x, key_weight = after((w_y, w_x, key_weight), two_b)
    more_wx = px(jnp.concatenate([key_weight[:late], w_y[:half]], axis=0))
    more_wy = py(jnp.concatenate([key_weight[early:], w_x[early - half :]], axis=0))
    total_a = total_of(pair_a, over_z(2)(pair_a))
    got_a = over_z(1)(total_a)
    local_b = after(own_rows(own_b, in_b, two_b), total_a)
    into_b = in_pair(*local_b)

    gain_rows = jnp.concatenate(
        [
            jnp.sum(v * widen(key_weight[n * quarter : (n + 1) * quarter]), axis=1)
            for n, v in enumerate((*local_a, *local_b))
        ]
    )
    bias = sum(jnp.sum(widen(v), axis=0) for v in (dproj, *dproj_sib))
    n_own = own // HEAD
    small = jnp.concatenate([gain_rows / my_gain, bias]).reshape(-1, HEAD)
    small = small + over_z(1)(small)
    into_b, small = after((into_b, small))
    pair_b = pair_sum(*local_b, into_b)
    small = small + over_z(2)(small)
    acts = (mine_a[3], mine_b[3], mine_a[1], mine_b[2], s_a3, s_b3, s_a1, rest)
    places = (
        (0, 4, 0, ((0, late, half),)),
        (1, 5, 0, ((1, late, half),)),
        (2, 6, 0, ((0, 0, late), (3, 0, half - late))),
        (3, 7, 3, ((2, half, early - half), (1, 0, late))),
    )
    more_wx, more_wy = after((more_wx, more_wy), pair_b)
    forwarded = forward(acts, places, (more_wx, more_wy, w_y, w_x), here)
    other_b, got_a, small, forwarded = after((over_z(2)(pair_b), got_a, small, forwarded))
    total_b = total_of(pair_b, other_b)
    got_b = over_z(1)(total_b)

    here, *there = forwarded
    keys = call(keys_body, jax.ShapeDtypeStruct((tok, kw), BF16), "keys")(
        here, *(core(v) for v in there), key_bias[None, :], cosine, sine
    )

    def ordered(first, one, two):
        return jnp.concatenate([jnp.where(first, one, two), jnp.where(first, two, one)], axis=0)

    gains, bias = small[:n_own], small[n_own:]
    gains = ordered(firsts[0], gains, core(gains))
    packed = jnp.concatenate([gains, bias], axis=0)
    n = gains.shape[0]
    got_x, got_y, got_xy = px(packed), py(packed), over(6)(packed)
    same = ordered(firsts[1], gains, got_x[:n])
    gains = ordered(firsts[2], same, ordered(firsts[1], got_y[:n], got_xy[:n]))
    bias = (bias + got_x[n:]) + (got_y[n:] + got_xy[n:])

    scale = 1.0 / jnp.sqrt(F32(tok * 32))
    got_b, keys, gains, bias = after((got_b, keys, gains, bias))
    grad = jnp.concatenate([*both(total_a, got_a), *both(total_b, got_b)], axis=0)
    return (keys, grad * scale, bias.reshape(-1) * scale, gains.reshape(-1) * scale)


def by_collectives(hidden_in, segment_ids, key_weight, norm_gain, key_bias, key_cotangent):
    tok_rows = hidden_in.shape[0]
    n_cycle = lax.axis_size("blk")
    n_rep = lax.axis_size("dp")
    positions = positions_of(segment_ids).reshape(tok_rows)
    xf = hidden_in.astype(F32)
    normed = xf * lax.rsqrt(jnp.mean(xf * xf, axis=1, keepdims=True) + 1e-06)
    scaled = (normed * norm_gain[None, :]).astype(BF16)
    cosine, sine = angles_of(positions, HEAD)
    dproj = rotate(key_cotangent.astype(F32), cosine, sine, -1.0).astype(BF16)
    full_weight = lax.all_gather(key_weight, "blk", axis=0, tiled=True)
    projected = jnp.dot(scaled, full_weight, preferred_element_type=F32)
    dscaled = lax.dot_general(
        dproj, full_weight, (((1,), (1,)), ((), ())), preferred_element_type=F32
    )
    projected = projected + key_bias[None, :]
    keys = rotate(projected, cosine, sine, 1.0).astype(BF16)
    cycle_part = lax.psum_scatter(
        lax.dot_general(scaled, dproj, (((0,), (0,)), ((), ())), preferred_element_type=F32),
        "blk",
        scatter_dimension=0,
        tiled=True,
    )
    grad_weight = lax.psum(cycle_part, "dp")
    bias_part = jnp.sum(dproj.astype(F32), axis=0)
    gain_part = jnp.sum(dscaled * normed, axis=0)
    grad_bias, grad_gain = lax.psum((bias_part, gain_part), ("blk", "dp"))
    scale = 1.0 / jnp.sqrt(F32(tok_rows * n_cycle * n_rep))
    return (keys, grad_weight * scale, grad_bias * scale, grad_gain * scale)


def solution(mesh):
    small = mesh.shape["blk"] == 8 and mesh.shape["dp"] == 4
    return jax.shard_map(
        by_permutes if small else by_collectives,
        mesh=mesh,
        in_specs=(
            P(("blk", "dp"), None),
            P(("blk", "dp"), None),
            P("blk", None),
            P(),
            P(),
            P(("blk", "dp"), None),
        ),
        out_specs=(P(("blk", "dp"), None), P("blk", None), P(), P()),
        check_vma=False,
    )
```

```python
import functools
import math

import jax
import jax.numpy as jnp
from jax import lax
from jax.experimental import pallas as pl
from jax.experimental.pallas import tpu as pltpu
from jax.sharding import PartitionSpec as P

KVH = 4
HEAD = 128
KW = 512
F32 = jnp.float32
BF16 = jnp.bfloat16


def positions_of(segs):
    same = segs[:, :, None] == segs[:, None, :]
    idx = jnp.arange(segs.shape[1], dtype=jnp.int32)
    earlier = idx[None, :] < idx[:, None]
    return jnp.sum((same & earlier[None]).astype(jnp.int32), axis=2)


def angles_of(pos, head):
    half = head // 2
    freq = jnp.arange(half, dtype=F32) * (2.0 / head)
    inv = jnp.power(F32(1000000.0), -freq)
    ang = pos.astype(F32)[:, None] * inv[None, :]
    return (jnp.cos(ang)[:, None, :], jnp.sin(ang)[:, None, :])


def rotate(values, cosine, sine, sign):
    rows = values.shape[0]
    heads = values.reshape(rows, KVH, HEAD)
    first = heads[:, :, : HEAD // 2]
    second = heads[:, :, HEAD // 2 :]
    out_a = first * cosine - sign * second * sine
    out_b = second * cosine + sign * first * sine
    return jnp.concatenate([out_a, out_b], axis=2).reshape(rows, KW)


def after(value, *others):
    return lax.optimization_barrier((value, *others))[0]


def call(body, out_shape, name, in_specs=None):
    return pl.pallas_call(
        body,
        out_shape=out_shape,
        **({} if in_specs is None else {"in_specs": in_specs}),
        cost_estimate=pl.CostEstimate(flops=1, bytes_accessed=1, transcendentals=0),
        compiler_params=pltpu.CompilerParams(vmem_limit_bytes=10 * 1024 * 1024),
        name=name,
    )


def turn(v, cosine, sine):
    return v * cosine + pltpu.roll(v, HEAD // 2, 1) * sine


def prepare_body(per_batch, at_ref, x_ref, gain_ref, seg_ref, cot_ref, *outs):
    step, wide = x_ref.shape
    part = wide // 8
    half = part // 2
    total = None
    for b in range(8):
        xb = x_ref[:, b * part : (b + 1) * part].astype(F32)
        add = jnp.sum(xb * xb, axis=1, keepdims=True)
        total = add if total is None else total + add
    inv = lax.rsqrt(total * (1.0 / wide) + 1e-06)
    me = at_ref[0]
    mine, sib, rest = outs[:8], outs[8:12], outs[12]
    cos_ref, sin_ref, dproj_ref, own_gain_ref = outs[13:]
    own_gain_ref[...] = gain_ref[:, pl.ds(pl.multiple_of(me * part, part), part)]
    places = {3: 0, 1: 1, 2: 2, 7: 3}
    for o in range(8):
        start = pl.multiple_of((me ^ o) * part, part)
        for chunk in range(2):
            cols = pl.ds(start + chunk * half, half)
            xb = x_ref[:, cols].astype(F32)
            done = (xb * inv * gain_ref[:, cols]).astype(BF16)
            at = 4 * chunk + o // 2
            if not o & 1:
                mine[at][...] = done
            elif at in places:
                sib[places[at]][...] = done
            else:
                at = max(at - 3, 0) * half
                rest[:, at : at + half] = done

    r = pl.program_id(0)
    seq = seg_ref.shape[1]
    segs = seg_ref[pl.ds(r // per_batch, 1), :]
    row = lax.broadcasted_iota(jnp.int32, (step, seq), 0) + r % per_batch * step
    col = lax.broadcasted_iota(jnp.int32, (step, seq), 1)
    own = jnp.sum(jnp.where(row == col, segs, 0), axis=1, keepdims=True)
    position = jnp.sum(
        jnp.where((own == segs) & (col < row), 1, 0), axis=1, keepdims=True
    )
    lane = lax.broadcasted_iota(jnp.int32, (1, HEAD), 1)
    second = lane >= HEAD // 2
    freq = (lane % (HEAD // 2)).astype(F32)
    angle = position.astype(F32) * jnp.exp(freq * (-2.0 * math.log(1000000.0) / HEAD))
    pair = jnp.cos(angle - jnp.where(second, math.pi / 2, 0.0).astype(F32))
    swapped = pltpu.roll(pair, HEAD // 2, 1)
    cosine = jnp.where(second, swapped, pair)
    sine = jnp.where(second, -pair, swapped)
    cos_ref[...] = cosine
    sin_ref[...] = sine
    for h in range(KVH):
        cols = slice(h * HEAD, (h + 1) * HEAD)
        dproj_ref[:, cols] = turn(cot_ref[:, cols].astype(F32), cosine, sine).astype(BF16)


def prepared(x, gain, segs, cotangent, at):
    rows, wide = x.shape
    step = 128
    half = wide // 16
    outs = [(half, BF16)] * 12 + [(4 * half, BF16), (HEAD, F32), (HEAD, F32), (KW, BF16)]
    def whole(v):
        return pl.BlockSpec(v.shape, lambda r, at: (0, 0))

    def some(n):
        return pl.BlockSpec((step, n), lambda r, at: (r, 0))

    x, gain, segs, cotangent = (
        pltpu.with_memory_space_constraint(v, pltpu.HBM)
        for v in (x, gain[None, :], segs, cotangent)
    )
    return pl.pallas_call(
        functools.partial(prepare_body, segs.shape[1] // step),
        grid_spec=pltpu.PrefetchScalarGridSpec(
            num_scalar_prefetch=1,
            grid=(rows // step,),
            in_specs=[some(wide), whole(gain), whole(segs), some(KW)],
            out_specs=[
                *(some(n) for n, _ in outs),
                pl.BlockSpec((1, 2 * half), lambda r, at: (0, 0)),
            ],
        ),
        out_shape=[
            *(jax.ShapeDtypeStruct((rows, n), t) for n, t in outs),
            jax.ShapeDtypeStruct((1, 2 * half), F32),
        ],
        cost_estimate=pl.CostEstimate(flops=1, bytes_accessed=1, transcendentals=0),
        compiler_params=pltpu.CompilerParams(vmem_limit_bytes=14 * 1024 * 1024),
        name="prepare",
    )(at, x, gain, segs, cotangent)


def keys_body(here, upper, middle, lower, bias, cos_ref, sin_ref, out_ref):
    for h in range(KVH):
        cols = slice(h * HEAD, (h + 1) * HEAD)
        there = jnp.concatenate([v[:, cols] for v in (upper, middle, lower)], axis=0).astype(F32)
        v = here[:, cols] + there + bias[:, cols]
        out_ref[:, cols] = turn(v, cos_ref[...], -sin_ref[...]).astype(BF16)


def product(mine, sib, dproj, dproj_sib):
    dims = (((0,), (0,)), ((), ()))
    return lax.dot_general(mine, dproj, dims, preferred_element_type=F32) + lax.dot_general(
        sib, dproj_sib, dims, preferred_element_type=F32
    )


def spread(rows, chip, outs):
    to_x, to_y, keep_y, keep_x = outs
    half = rows.shape[0] // 2
    low = {1: (to_x, 0), 3: (to_x, half), 2: (keep_y, 0)}[chip]
    high = {2: (to_y, 0), 3: (to_y, half), 1: (keep_x, 0)}[chip]
    for (ref, at), part in ((low, rows[:half]), (high, rows[half:])):
        ref[at : at + half] = part.astype(ref.dtype)


def first_grad_body(m1, m2, m3, s1, s2, s3, dproj, upper, lower, *outs):
    dproj_sib = jnp.concatenate([upper[...], lower[...]], axis=0)
    for chip, mine, sib in ((3, m3, s3), (1, m1, s1), (2, m2, s2)):
        spread(product(mine[...], sib[...], dproj[...], dproj_sib), chip, outs)


def second_grad_body(m_a0, m0, m1, m2, m3, s3, rest, dproj, upper, lower, own_a, own_b, *outs):
    dproj_sib = jnp.concatenate([upper[...], lower[...]], axis=0)
    half = m0.shape[1]
    own_a[...] = product(m_a0[...], rest[:, :half], dproj[...], dproj_sib)
    for chip, mine in ((3, m3), (1, m1), (2, m2), (0, m0)):
        sib = s3[...] if chip == 3 else rest[:, (chip + 1) * half : (chip + 2) * half]
        rows = product(mine[...], sib, dproj[...], dproj_sib)
        if chip:
            spread(rows, chip, outs)
        else:
            own_b[...] = rows


def forward_body(places, n_acts, n_init, *refs):
    acts, init, refs = refs[:n_acts], refs[n_acts : n_acts + n_init], refs[n_acts + n_init :]
    half = acts[0].shape[1]
    n_outs = 4 if n_init else 2
    weights, outs = refs[:-n_outs], refs[-n_outs:]
    totals = [v[...] for v in init] if n_init else [None, None]
    for side in (1, 0):
        total = totals[side]
        for mine, sib, col, pieces in places:
            w = jnp.concatenate([weights[n][at : at + rows] for n, at, rows in pieces], axis=0)
            rows = acts[sib][:, col * half : (col + 1) * half] if side else acts[mine][...]
            add = jnp.dot(rows, w, preferred_element_type=F32)
            total = add if total is None else total + add
        if side and n_init:
            start = 0
            for out in outs[1:]:
                stop = start + out.shape[0]
                out[...] = total[start:stop].astype(BF16)
                start = stop
        else:
            outs[side][...] = total


def forward(acts, places, weights, init=()):
    tok, kw = acts[0].shape[0], weights[0].shape[1]
    shape = jax.ShapeDtypeStruct((tok, kw), F32)
    third = tok // 48 * 16
    parts = [jax.ShapeDtypeStruct((n, kw), BF16) for n in (third, third, tok - 2 * third)]
    return call(
        functools.partial(forward_body, places, len(acts), len(init)),
        [shape, *parts] if init else [shape, shape],
        "forward",
    )(*acts, *init, *weights)


def collect_body(scale, at_ref, here, over_x, over_y, over_xy, gains_ref, bias_ref):
    n = gains_ref.shape[0] // 8
    chip, core = at_ref[0] // 2, at_ref[0] % 2
    refs = (here, over_x, over_y, over_xy)
    for away, ref in enumerate(refs):
        first = (chip ^ away) * 2
        gains_ref[pl.ds(pl.multiple_of((first + core) * n, n), n)] = ref[:n] * scale
        gains_ref[pl.ds(pl.multiple_of((first + 1 - core) * n, n), n)] = ref[n : 2 * n] * scale
    bias = [ref[2 * n :] for ref in refs]
    bias_ref[...] = ((bias[0] + bias[1]) + (bias[2] + bias[3])) * scale


def by_permutes(hidden_in, segment_ids, key_weight, norm_gain, key_bias, key_cotangent):
    tok = hidden_in.shape[0]
    me = lax.axis_index("blk")
    own, kw = key_weight.shape
    half = own // 2
    quarter = own // 4

    def over(bit):
        return lambda v: lax.ppermute(v, "blk", [(i, i ^ bit) for i in range(8)])

    core, px, py = over(1), over(2), over(4)

    def widen(v):
        return v.astype(F32)

    odd = (lax.axis_index("dp") & 1) == 1
    at = me.reshape(1).astype(jnp.int32)
    odd, at, key_weight, hidden_in, key_cotangent, segment_ids = after(
        (odd, at, key_weight, hidden_in, key_cotangent, segment_ids)
    )
    early = half + own*17//64
    late = own - early
    w_x, w_y = px(key_weight[late:]), py(key_weight[:early])

    parts = prepared(hidden_in, norm_gain, segment_ids, key_cotangent, at)
    mine_a, mine_b, (s_a3, s_a1, s_a2, s_b3, rest) = parts[:4], parts[4:8], parts[8:13]
    cosine, sine, dproj, my_gain = parts[13:]
    my_gain = my_gain.reshape(own)
    n = tok // 2
    dproj_sib = core(dproj[:n]), core(dproj[n:])
    s_a3, s_a1, s_a2 = core(s_a3), core(s_a1), core(s_a2)

    def part_shapes(h):
        shapes = ((2 * h, BF16), (2 * h, BF16), (h, BF16), (h, BF16))
        return [jax.ShapeDtypeStruct((r, kw), t) for r, t in shapes]

    def add_up(part, from_x, from_y):
        _, _, keep_y, keep_x = part
        more_y = (widen(keep_y) + widen(from_x[quarter:])).astype(BF16)
        more_x = (widen(keep_x) + widen(from_y[quarter:])).astype(BF16)
        return more_y, more_x

    def own_rows(mine, first, second):
        low = mine[:quarter] + widen(first[0][:quarter]) + widen(second[0])
        high = mine[quarter:] + widen(first[1][:quarter]) + widen(second[1])
        return low, high

    def over_z(bit):
        return lambda v: lax.ppermute(v, "dp", [(i, i ^ bit) for i in range(4)])

    def in_pair(low, high):
        sent = jnp.where(odd, low, high).astype(BF16)
        return over_z(1)(sent)

    def pair_sum(low, high, into):
        return (jnp.where(odd, high, low) + widen(into)).astype(BF16)

    def total_of(pair, other):
        return (widen(pair) + widen(other)).astype(BF16)

    def both(total, got):
        return widen(jnp.where(odd, got, total)), widen(jnp.where(odd, total, got))

    part_a = call(first_grad_body, part_shapes(quarter), "grad_a")(
        *mine_a[1:], s_a1, s_a2, s_a3, dproj, *dproj_sib
    )
    to_a = after((part_a[0], part_a[1]), w_x, w_y)
    in_a = px(to_a[0]), py(to_a[1])
    s_b3, rest = after((s_b3, rest), part_a, w_x, w_y)
    s_b3, rest = core(s_b3), core(rest)
    own_shape = jax.ShapeDtypeStruct((half, kw), F32)
    own_a, own_b, *part_b = call(
        second_grad_body, [own_shape, own_shape, *part_shapes(quarter)], "grad_b"
    )(mine_a[0], *mine_b, s_b3, rest, dproj, *dproj_sib)

    acts = (mine_a[0], mine_b[0], mine_a[2], mine_b[1], s_a2, rest)
    places = (
        (0, 5, 0, ((0, 0, half),)),
        (1, 5, 1, ((0, half, half),)),
        (2, 4, 0, ((1, 0, half),)),
        (3, 5, 2, ((2, early - half, half),)),
    )
    here = forward(acts, places, (after(key_weight, part_b), w_y, w_x))

    in_a = after(in_a, here)
    to_b = after((part_b[0], part_b[1]), in_a)
    more = add_up(part_a, *in_a)
    two_a = py(more[0]), px(more[1])
    in_b = px(to_b[0]), py(to_b[1])
    local_a = own_rows(own_a, in_a, two_a)
    pair_a = pair_sum(*local_a, in_pair(*local_a))

    in_b = after(in_b, two_a)
    more = add_up(part_b, *in_b)
    two_b = py(more[0]), px(more[1])
    w_y, w_x, key_weight = after((w_y, w_x, key_weight), two_b)
    more_wx = px(jnp.concatenate([key_weight[:late], w_y[:half]], axis=0))
    more_wy = py(jnp.concatenate([key_weight[early:], w_x[early - half :]], axis=0))
    total_a = total_of(pair_a, over_z(2)(pair_a))
    got_a = over_z(1)(total_a)
    local_b = after(own_rows(own_b, in_b, two_b), total_a)
    into_b = in_pair(*local_b)

    gain_rows = jnp.concatenate(
        [
            jnp.sum(v * widen(key_weight[n * quarter : (n + 1) * quarter]), axis=1)
            for n, v in enumerate((*local_a, *local_b))
        ]
    )
    bias = sum(jnp.sum(widen(v), axis=0) for v in (dproj, *dproj_sib))
    n_own = own // HEAD
    small = jnp.concatenate([gain_rows / my_gain, bias]).reshape(-1, HEAD)
    small = small + over_z(1)(small)
    into_b, small = after((into_b, small))
    pair_b = pair_sum(*local_b, into_b)
    small = small + over_z(2)(small)
    acts = (mine_a[3], mine_b[3], mine_a[1], mine_b[2], s_a3, s_b3, s_a1, rest)
    places = (
        (0, 4, 0, ((0, late, half),)),
        (1, 5, 0, ((1, late, half),)),
        (2, 6, 0, ((0, 0, late), (3, 0, half - late))),
        (3, 7, 3, ((2, half, early - half), (1, 0, late))),
    )
    gains, bias = small[:n_own], small[n_own:]
    other_gains = core(gains)
    other_b, got_a, gains, bias, other_gains, more_wx, more_wy = after(
        (over_z(2)(pair_b), got_a, gains, bias, other_gains, more_wx, more_wy)
    )
    total_b = total_of(pair_b, other_b)
    got_b = over_z(1)(total_b)
    more_wx, more_wy = after((more_wx, more_wy), total_b)
    forwarded = forward(acts, places, (more_wx, more_wy, w_y, w_x), here)

    here, *there = forwarded
    keys = call(keys_body, jax.ShapeDtypeStruct((tok, kw), BF16), "keys")(
        here, *(core(v) for v in there), key_bias[None, :], cosine, sine
    )

    scale = 1.0 / math.sqrt(tok * 32)
    packed = jnp.concatenate([gains, other_gains, bias], axis=0)
    gains, bias = call(
        functools.partial(collect_body, scale),
        [
            jax.ShapeDtypeStruct((8 * n_own, HEAD), F32),
            jax.ShapeDtypeStruct(bias.shape, F32),
        ],
        "collect",
        [pl.BlockSpec(memory_space=pltpu.SMEM)] + [pl.BlockSpec(memory_space=pltpu.VMEM)] * 4,
    )(at, packed, px(packed), py(packed), over(6)(packed))

    got_b, keys = after((got_b, keys))
    grad = jnp.concatenate([*both(total_a, got_a), *both(total_b, got_b)], axis=0)
    return (keys, grad * scale, bias.reshape(-1), gains.reshape(-1))


def by_collectives(hidden_in, segment_ids, key_weight, norm_gain, key_bias, key_cotangent):
    tok_rows = hidden_in.shape[0]
    n_cycle = lax.axis_size("blk")
    n_rep = lax.axis_size("dp")
    positions = positions_of(segment_ids).reshape(tok_rows)
    xf = hidden_in.astype(F32)
    normed = xf * lax.rsqrt(jnp.mean(xf * xf, axis=1, keepdims=True) + 1e-06)
    scaled = (normed * norm_gain[None, :]).astype(BF16)
    cosine, sine = angles_of(positions, HEAD)
    dproj = rotate(key_cotangent.astype(F32), cosine, sine, -1.0).astype(BF16)
    full_weight = lax.all_gather(key_weight, "blk", axis=0, tiled=True)
    projected = jnp.dot(scaled, full_weight, preferred_element_type=F32)
    dscaled = lax.dot_general(
        dproj, full_weight, (((1,), (1,)), ((), ())), preferred_element_type=F32
    )
    projected = projected + key_bias[None, :]
    keys = rotate(projected, cosine, sine, 1.0).astype(BF16)
    cycle_part = lax.psum_scatter(
        lax.dot_general(scaled, dproj, (((0,), (0,)), ((), ())), preferred_element_type=F32),
        "blk",
        scatter_dimension=0,
        tiled=True,
    )
    grad_weight = lax.psum(cycle_part, "dp")
    bias_part = jnp.sum(dproj.astype(F32), axis=0)
    gain_part = jnp.sum(dscaled * normed, axis=0)
    grad_bias, grad_gain = lax.psum((bias_part, gain_part), ("blk", "dp"))
    scale = 1.0 / jnp.sqrt(F32(tok_rows * n_cycle * n_rep))
    return (keys, grad_weight * scale, grad_bias * scale, grad_gain * scale)


def solution(mesh):
    small = mesh.shape["blk"] == 8 and mesh.shape["dp"] == 4
    return jax.shard_map(
        by_permutes if small else by_collectives,
        mesh=mesh,
        in_specs=(
            P(("blk", "dp"), None),
            P(("blk", "dp"), None),
            P("blk", None),
            P(),
            P(),
            P(("blk", "dp"), None),
        ),
        out_specs=(P(("blk", "dp"), None), P("blk", None), P(), P()),
        check_vma=False,
    )
```

```python
import functools
import math

import jax
import jax.numpy as jnp
from jax import lax
from jax.experimental import pallas as pl
from jax.experimental.pallas import tpu as pltpu
from jax.sharding import PartitionSpec as P

KVH = 4
HEAD = 128
KW = 512
F32 = jnp.float32
BF16 = jnp.bfloat16


def positions_of(segs):
    same = segs[:, :, None] == segs[:, None, :]
    idx = jnp.arange(segs.shape[1], dtype=jnp.int32)
    earlier = idx[None, :] < idx[:, None]
    return jnp.sum((same & earlier[None]).astype(jnp.int32), axis=2)


def angles_of(pos, head):
    half = head // 2
    freq = jnp.arange(half, dtype=F32) * (2.0 / head)
    inv = jnp.power(F32(1000000.0), -freq)
    ang = pos.astype(F32)[:, None] * inv[None, :]
    return (jnp.cos(ang)[:, None, :], jnp.sin(ang)[:, None, :])


def rotate(values, cosine, sine, sign):
    rows = values.shape[0]
    heads = values.reshape(rows, KVH, HEAD)
    first = heads[:, :, : HEAD // 2]
    second = heads[:, :, HEAD // 2 :]
    out_a = first * cosine - sign * second * sine
    out_b = second * cosine + sign * first * sine
    return jnp.concatenate([out_a, out_b], axis=2).reshape(rows, KW)


def after(value, *others):
    return lax.optimization_barrier((value, *others))[0]


def call(body, out_shape, name, in_specs=None):
    return pl.pallas_call(
        body,
        out_shape=out_shape,
        **({} if in_specs is None else {"in_specs": in_specs}),
        cost_estimate=pl.CostEstimate(flops=1, bytes_accessed=1, transcendentals=0),
        compiler_params=pltpu.CompilerParams(vmem_limit_bytes=10 * 1024 * 1024),
        name=name,
    )


def turn(v, cosine, sine):
    return v * cosine + pltpu.roll(v, HEAD // 2, 1) * sine


def prepare_body(per_batch, at_ref, x_ref, gain_ref, seg_ref, cot_ref, *outs):
    step, wide = x_ref.shape
    part = wide // 8
    half = part // 2
    total = None
    for b in range(8):
        xb = x_ref[:, b * part : (b + 1) * part].astype(F32)
        add = jnp.sum(xb * xb, axis=1, keepdims=True)
        total = add if total is None else total + add
    inv = lax.rsqrt(total * (1.0 / wide) + 1e-06)
    me = at_ref[0]
    mine, sib, rest = outs[:8], outs[8:12], outs[12]
    cos_ref, sin_ref, dproj_ref, own_gain_ref = outs[13:]
    own_gain_ref[...] = gain_ref[:, pl.ds(pl.multiple_of(me * part, part), part)]
    places = {3: 0, 1: 1, 2: 2, 7: 3}
    for o in range(8):
        start = pl.multiple_of((me ^ o) * part, part)
        for chunk in range(2):
            cols = pl.ds(start + chunk * half, half)
            xb = x_ref[:, cols].astype(F32)
            done = (xb * inv * gain_ref[:, cols]).astype(BF16)
            at = 4 * chunk + o // 2
            if not o & 1:
                mine[at][...] = done
            elif at in places:
                sib[places[at]][...] = done
            else:
                at = max(at - 3, 0) * half
                rest[:, at : at + half] = done

    r = pl.program_id(0)
    seq = seg_ref.shape[1]
    segs = seg_ref[pl.ds(r // per_batch, 1), :]
    row = lax.broadcasted_iota(jnp.int32, (step, seq), 0) + r % per_batch * step
    col = lax.broadcasted_iota(jnp.int32, (step, seq), 1)
    own = jnp.sum(jnp.where(row == col, segs, 0), axis=1, keepdims=True)
    position = jnp.sum(
        jnp.where((own == segs) & (col < row), 1, 0), axis=1, keepdims=True
    )
    lane = lax.broadcasted_iota(jnp.int32, (1, HEAD), 1)
    second = lane >= HEAD // 2
    freq = (lane % (HEAD // 2)).astype(F32)
    angle = position.astype(F32) * jnp.exp(freq * (-2.0 * math.log(1000000.0) / HEAD))
    pair = jnp.cos(angle - jnp.where(second, math.pi / 2, 0.0).astype(F32))
    swapped = pltpu.roll(pair, HEAD // 2, 1)
    cosine = jnp.where(second, swapped, pair)
    sine = jnp.where(second, -pair, swapped)
    cos_ref[...] = cosine
    sin_ref[...] = sine
    for h in range(KVH):
        cols = slice(h * HEAD, (h + 1) * HEAD)
        dproj_ref[:, cols] = turn(cot_ref[:, cols].astype(F32), cosine, sine).astype(BF16)


def prepared(x, gain, segs, cotangent, at):
    rows, wide = x.shape
    step = 128
    half = wide // 16
    outs = [(half, BF16)] * 12 + [(4 * half, BF16), (HEAD, F32), (HEAD, F32), (KW, BF16)]
    def whole(v):
        return pl.BlockSpec(v.shape, lambda r, at: (0, 0))

    def some(n):
        return pl.BlockSpec((step, n), lambda r, at: (r, 0))

    x, gain, segs, cotangent = (
        pltpu.with_memory_space_constraint(v, pltpu.HBM)
        for v in (x, gain[None, :], segs, cotangent)
    )
    return pl.pallas_call(
        functools.partial(prepare_body, segs.shape[1] // step),
        grid_spec=pltpu.PrefetchScalarGridSpec(
            num_scalar_prefetch=1,
            grid=(rows // step,),
            in_specs=[some(wide), whole(gain), whole(segs), some(KW)],
            out_specs=[
                *(some(n) for n, _ in outs),
                pl.BlockSpec((1, 2 * half), lambda r, at: (0, 0)),
            ],
        ),
        out_shape=[
            *(jax.ShapeDtypeStruct((rows, n), t) for n, t in outs),
            jax.ShapeDtypeStruct((1, 2 * half), F32),
        ],
        cost_estimate=pl.CostEstimate(flops=1, bytes_accessed=1, transcendentals=0),
        compiler_params=pltpu.CompilerParams(vmem_limit_bytes=14 * 1024 * 1024),
        name="prepare",
    )(at, x, gain, segs, cotangent)


def keys_body(here, upper, middle, lower, bias, cos_ref, sin_ref, out_ref):
    for h in range(KVH):
        cols = slice(h * HEAD, (h + 1) * HEAD)
        there = jnp.concatenate([v[:, cols] for v in (upper, middle, lower)], axis=0).astype(F32)
        v = here[:, cols] + there + bias[:, cols]
        out_ref[:, cols] = turn(v, cos_ref[...], -sin_ref[...]).astype(BF16)


def product(mine, sib, dproj, dproj_sib):
    dims = (((0,), (0,)), ((), ()))
    return lax.dot_general(mine, dproj, dims, preferred_element_type=F32) + lax.dot_general(
        sib, dproj_sib, dims, preferred_element_type=F32
    )


def spread(rows, chip, outs):
    to_x, to_y, keep_y, keep_x = outs
    half = rows.shape[0] // 2
    low = {1: (to_x, 0), 3: (to_x, half), 2: (keep_y, 0)}[chip]
    high = {2: (to_y, 0), 3: (to_y, half), 1: (keep_x, 0)}[chip]
    for (ref, at), part in ((low, rows[:half]), (high, rows[half:])):
        ref[at : at + half] = part.astype(ref.dtype)


def first_grad_body(m1, m2, m3, s1, s2, s3, dproj, upper, middle, lower, *outs):
    dproj_sib = jnp.concatenate([upper[...], middle[...], lower[...]], axis=0)
    for chip, mine, sib in ((3, m3, s3), (1, m1, s1), (2, m2, s2)):
        spread(product(mine[...], sib[...], dproj[...], dproj_sib), chip, outs)


def second_grad_body(m_a0, m0, m1, m2, m3, s3, rest, dproj, upper, middle, lower, own_a, own_b, *outs):
    dproj_sib = jnp.concatenate([upper[...], middle[...], lower[...]], axis=0)
    half = m0.shape[1]
    own_a[...] = product(m_a0[...], rest[:, :half], dproj[...], dproj_sib)
    for chip, mine in ((3, m3), (1, m1), (2, m2), (0, m0)):
        sib = s3[...] if chip == 3 else rest[:, (chip + 1) * half : (chip + 2) * half]
        rows = product(mine[...], sib, dproj[...], dproj_sib)
        if chip:
            spread(rows, chip, outs)
        else:
            own_b[...] = rows


def forward_body(places, n_acts, n_init, *refs):
    acts, init, refs = refs[:n_acts], refs[n_acts : n_acts + n_init], refs[n_acts + n_init :]
    half = acts[0].shape[1]
    n_outs = 4 if n_init else 2
    weights, outs = refs[:-n_outs], refs[-n_outs:]
    totals = [v[...] for v in init] if n_init else [None, None]
    for side in (1, 0):
        total = totals[side]
        for mine, sib, col, pieces in places:
            w = jnp.concatenate([weights[n][at : at + rows] for n, at, rows in pieces], axis=0)
            rows = acts[sib][:, col * half : (col + 1) * half] if side else acts[mine][...]
            add = jnp.dot(rows, w, preferred_element_type=F32)
            total = add if total is None else total + add
        if side and n_init:
            start = 0
            for out in outs[1:]:
                stop = start + out.shape[0]
                out[...] = total[start:stop].astype(BF16)
                start = stop
        else:
            outs[side][...] = total


def forward(acts, places, weights, init=()):
    tok, kw = acts[0].shape[0], weights[0].shape[1]
    shape = jax.ShapeDtypeStruct((tok, kw), F32)
    third = tok // 48 * 16
    parts = [jax.ShapeDtypeStruct((n, kw), BF16) for n in (third, third, tok - 2 * third)]
    return call(
        functools.partial(forward_body, places, len(acts), len(init)),
        [shape, *parts] if init else [shape, shape],
        "forward",
    )(*acts, *init, *weights)


def collect_body(scale, at_ref, here, over_x, over_y, over_xy, gains_ref, bias_ref):
    n = gains_ref.shape[0] // 8
    chip, core = at_ref[0] // 2, at_ref[0] % 2
    refs = (here, over_x, over_y, over_xy)
    for away, ref in enumerate(refs):
        first = (chip ^ away) * 2
        gains_ref[pl.ds(pl.multiple_of((first + core) * n, n), n)] = ref[:n] * scale
        gains_ref[pl.ds(pl.multiple_of((first + 1 - core) * n, n), n)] = ref[n : 2 * n] * scale
    bias = [ref[2 * n :] for ref in refs]
    bias_ref[...] = ((bias[0] + bias[1]) + (bias[2] + bias[3])) * scale


def by_permutes(hidden_in, segment_ids, key_weight, norm_gain, key_bias, key_cotangent):
    tok = hidden_in.shape[0]
    me = lax.axis_index("blk")
    own, kw = key_weight.shape
    half = own // 2
    quarter = own // 4

    def over(bit):
        return lambda v: lax.ppermute(v, "blk", [(i, i ^ bit) for i in range(8)])

    core, px, py = over(1), over(2), over(4)

    def widen(v):
        return v.astype(F32)

    odd = (lax.axis_index("dp") & 1) == 1
    at = me.reshape(1).astype(jnp.int32)
    odd, at, key_weight, hidden_in, key_cotangent, segment_ids = after(
        (odd, at, key_weight, hidden_in, key_cotangent, segment_ids)
    )
    early = half + own * 3 // 16
    late = own - early
    w_x, w_y = px(key_weight[late:]), py(key_weight[:early])

    parts = prepared(hidden_in, norm_gain, segment_ids, key_cotangent, at)
    mine_a, mine_b, (s_a3, s_a1, s_a2, s_b3, rest) = parts[:4], parts[4:8], parts[8:13]
    cosine, sine, dproj, my_gain = parts[13:]
    my_gain = my_gain.reshape(own)
    third = tok // 48 * 16
    cuts = (0, third, 2 * third, tok)
    dproj_sib = [core(dproj[i:j]) for i, j in zip(cuts[:-1], cuts[1:], strict=True)]
    s_a3, s_a1, s_a2 = core(s_a3), core(s_a1), core(s_a2)

    def part_shapes(h):
        shapes = ((2 * h, BF16), (2 * h, BF16), (h, BF16), (h, BF16))
        return [jax.ShapeDtypeStruct((r, kw), t) for r, t in shapes]

    def add_up(part, from_x, from_y):
        _, _, keep_y, keep_x = part
        more_y = (widen(keep_y) + widen(from_x[quarter:])).astype(BF16)
        more_x = (widen(keep_x) + widen(from_y[quarter:])).astype(BF16)
        return more_y, more_x

    def own_rows(mine, first, second):
        low = mine[:quarter] + widen(first[0][:quarter]) + widen(second[0])
        high = mine[quarter:] + widen(first[1][:quarter]) + widen(second[1])
        return low, high

    def over_z(bit):
        return lambda v: lax.ppermute(v, "dp", [(i, i ^ bit) for i in range(4)])

    def in_pair(low, high):
        sent = jnp.where(odd, low, high).astype(BF16)
        return over_z(1)(sent)

    def pair_sum(low, high, into):
        return (jnp.where(odd, high, low) + widen(into)).astype(BF16)

    def total_of(pair, other):
        return (widen(pair) + widen(other)).astype(BF16)

    def both(total, got):
        return widen(jnp.where(odd, got, total)), widen(jnp.where(odd, total, got))

    part_a = call(first_grad_body, part_shapes(quarter), "grad_a")(
        *mine_a[1:], s_a1, s_a2, s_a3, dproj, *dproj_sib
    )
    to_a = after((part_a[0], part_a[1]), w_x, w_y)
    in_a = px(to_a[0]), py(to_a[1])
    s_b3, rest = after((s_b3, rest), part_a, w_x, w_y)
    s_b3, rest = core(s_b3), core(rest)
    own_shape = jax.ShapeDtypeStruct((half, kw), F32)
    own_a, own_b, *part_b = call(
        second_grad_body, [own_shape, own_shape, *part_shapes(quarter)], "grad_b"
    )(mine_a[0], *mine_b, s_b3, rest, dproj, *dproj_sib)

    acts = (mine_a[0], mine_b[0], mine_a[2], mine_b[1], s_a2, rest)
    places = (
        (0, 5, 0, ((0, 0, half),)),
        (1, 5, 1, ((0, half, half),)),
        (2, 4, 0, ((1, 0, half),)),
        (3, 5, 2, ((2, early - half, half),)),
    )
    here = forward(acts, places, (after(key_weight, part_b), w_y, w_x))

    in_a = after(in_a, here)
    to_b = after((part_b[0], part_b[1]), in_a)
    more = add_up(part_a, *in_a)
    two_a = py(more[0]), px(more[1])
    in_b = px(to_b[0]), py(to_b[1])
    local_a = own_rows(own_a, in_a, two_a)
    pair_a = pair_sum(*local_a, in_pair(*local_a))

    in_b = after(in_b, two_a)
    more = add_up(part_b, *in_b)
    two_b = py(more[0]), px(more[1])
    w_y, w_x, key_weight = after((w_y, w_x, key_weight), two_b)
    more_wx = px(jnp.concatenate([key_weight[:late], w_y[:half]], axis=0))
    more_wy = py(jnp.concatenate([key_weight[early:], w_x[early - half :]], axis=0))
    total_a = total_of(pair_a, over_z(2)(pair_a))
    got_a = over_z(1)(total_a)
    local_b = after(own_rows(own_b, in_b, two_b), total_a)
    into_b = in_pair(*local_b)

    gain_rows = jnp.concatenate(
        [
            jnp.sum(v * widen(key_weight[n * quarter : (n + 1) * quarter]), axis=1)
            for n, v in enumerate((*local_a, *local_b))
        ]
    )
    bias = sum(jnp.sum(widen(v), axis=0) for v in (dproj, *dproj_sib))
    n_own = own // HEAD
    small = jnp.concatenate([gain_rows / my_gain, bias]).reshape(-1, HEAD)
    small = small + over_z(1)(small)
    into_b, small = after((into_b, small))
    pair_b = pair_sum(*local_b, into_b)
    small = small + over_z(2)(small)
    acts = (mine_a[3], mine_b[3], mine_a[1], mine_b[2], s_a3, s_b3, s_a1, rest)
    places = (
        (0, 4, 0, ((0, late, half),)),
        (1, 5, 0, ((1, late, half),)),
        (2, 6, 0, ((0, 0, late), (3, 0, half - late))),
        (3, 7, 3, ((2, half, early - half), (1, 0, late))),
    )
    gains, bias = small[:n_own], small[n_own:]
    other_gains = core(gains)
    other_b, got_a, gains, bias, other_gains, more_wx, more_wy = after(
        (over_z(2)(pair_b), got_a, gains, bias, other_gains, more_wx, more_wy)
    )
    total_b = total_of(pair_b, other_b)
    got_b = over_z(1)(total_b)
    more_wx, more_wy = after((more_wx, more_wy), total_b)
    forwarded = forward(acts, places, (more_wx, more_wy, w_y, w_x), here)

    here, *there = forwarded
    keys = call(keys_body, jax.ShapeDtypeStruct((tok, kw), BF16), "keys")(
        here, *(core(v) for v in there), key_bias[None, :], cosine, sine
    )

    scale = 1.0 / math.sqrt(tok * 32)
    packed = jnp.concatenate([gains, other_gains, bias], axis=0)
    gains, bias = call(
        functools.partial(collect_body, scale),
        [
            jax.ShapeDtypeStruct((8 * n_own, HEAD), F32),
            jax.ShapeDtypeStruct(bias.shape, F32),
        ],
        "collect",
        [pl.BlockSpec(memory_space=pltpu.SMEM)] + [pl.BlockSpec(memory_space=pltpu.VMEM)] * 4,
    )(at, packed, px(packed), py(packed), over(6)(packed))

    got_b, keys = after((got_b, keys))
    grad = jnp.concatenate([*both(total_a, got_a), *both(total_b, got_b)], axis=0)
    return (keys, grad * scale, bias.reshape(-1), gains.reshape(-1))


def by_collectives(hidden_in, segment_ids, key_weight, norm_gain, key_bias, key_cotangent):
    tok_rows = hidden_in.shape[0]
    n_cycle = lax.axis_size("blk")
    n_rep = lax.axis_size("dp")
    positions = positions_of(segment_ids).reshape(tok_rows)
    xf = hidden_in.astype(F32)
    normed = xf * lax.rsqrt(jnp.mean(xf * xf, axis=1, keepdims=True) + 1e-06)
    scaled = (normed * norm_gain[None, :]).astype(BF16)
    cosine, sine = angles_of(positions, HEAD)
    dproj = rotate(key_cotangent.astype(F32), cosine, sine, -1.0).astype(BF16)
    full_weight = lax.all_gather(key_weight, "blk", axis=0, tiled=True)
    projected = jnp.dot(scaled, full_weight, preferred_element_type=F32)
    dscaled = lax.dot_general(
        dproj, full_weight, (((1,), (1,)), ((), ())), preferred_element_type=F32
    )
    projected = projected + key_bias[None, :]
    keys = rotate(projected, cosine, sine, 1.0).astype(BF16)
    cycle_part = lax.psum_scatter(
        lax.dot_general(scaled, dproj, (((0,), (0,)), ((), ())), preferred_element_type=F32),
        "blk",
        scatter_dimension=0,
        tiled=True,
    )
    grad_weight = lax.psum(cycle_part, "dp")
    bias_part = jnp.sum(dproj.astype(F32), axis=0)
    gain_part = jnp.sum(dscaled * normed, axis=0)
    grad_bias, grad_gain = lax.psum((bias_part, gain_part), ("blk", "dp"))
    scale = 1.0 / jnp.sqrt(F32(tok_rows * n_cycle * n_rep))
    return (keys, grad_weight * scale, grad_bias * scale, grad_gain * scale)


def solution(mesh):
    small = mesh.shape["blk"] == 8 and mesh.shape["dp"] == 4
    return jax.shard_map(
        by_permutes if small else by_collectives,
        mesh=mesh,
        in_specs=(
            P(("blk", "dp"), None),
            P(("blk", "dp"), None),
            P("blk", None),
            P(),
            P(),
            P(("blk", "dp"), None),
        ),
        out_specs=(P(("blk", "dp"), None), P("blk", None), P(), P()),
        check_vma=False,
    )
```

```python
import functools
import math

import jax
import jax.numpy as jnp
from jax import lax
from jax.experimental import pallas as pl
from jax.experimental.pallas import tpu as pltpu
from jax.sharding import PartitionSpec as P

KVH = 4
HEAD = 128
KW = 512
F32 = jnp.float32
BF16 = jnp.bfloat16


def positions_of(segs):
    same = segs[:, :, None] == segs[:, None, :]
    idx = jnp.arange(segs.shape[1], dtype=jnp.int32)
    earlier = idx[None, :] < idx[:, None]
    return jnp.sum((same & earlier[None]).astype(jnp.int32), axis=2)


def angles_of(pos, head):
    half = head // 2
    freq = jnp.arange(half, dtype=F32) * (2.0 / head)
    inv = jnp.power(F32(1000000.0), -freq)
    ang = pos.astype(F32)[:, None] * inv[None, :]
    return (jnp.cos(ang)[:, None, :], jnp.sin(ang)[:, None, :])


def rotate(values, cosine, sine, sign):
    rows = values.shape[0]
    heads = values.reshape(rows, KVH, HEAD)
    first = heads[:, :, : HEAD // 2]
    second = heads[:, :, HEAD // 2 :]
    out_a = first * cosine - sign * second * sine
    out_b = second * cosine + sign * first * sine
    return jnp.concatenate([out_a, out_b], axis=2).reshape(rows, KW)


def after(value, *others):
    return lax.optimization_barrier((value, *others))[0]


def call(body, out_shape, name, in_specs=None):
    return pl.pallas_call(
        body,
        out_shape=out_shape,
        **({} if in_specs is None else {"in_specs": in_specs}),
        cost_estimate=pl.CostEstimate(flops=1, bytes_accessed=1, transcendentals=0),
        compiler_params=pltpu.CompilerParams(vmem_limit_bytes=10 * 1024 * 1024),
        name=name,
    )


def turn(v, cosine, sine):
    return v * cosine + pltpu.roll(v, HEAD // 2, 1) * sine


def prepare_body(per_batch, at_ref, x_ref, gain_ref, seg_ref, cot_ref, *outs):
    step, wide = x_ref.shape
    part = wide // 8
    half = part // 2
    total = None
    for b in range(8):
        xb = x_ref[:, b * part : (b + 1) * part].astype(F32)
        add = jnp.sum(xb * xb, axis=1, keepdims=True)
        total = add if total is None else total + add
    inv = lax.rsqrt(total * (1.0 / wide) + 1e-06)
    me = at_ref[0]
    mine, sib, rest = outs[:8], outs[8:12], outs[12]
    cos_ref, sin_ref, dproj_ref, own_gain_ref = outs[13:]
    own_gain_ref[...] = gain_ref[:, pl.ds(pl.multiple_of(me * part, part), part)]
    places = {3: 0, 1: 1, 2: 2, 7: 3}
    for o in range(8):
        start = pl.multiple_of((me ^ o) * part, part)
        for chunk in range(2):
            cols = pl.ds(start + chunk * half, half)
            xb = x_ref[:, cols].astype(F32)
            done = (xb * inv * gain_ref[:, cols]).astype(BF16)
            at = 4 * chunk + o // 2
            if not o & 1:
                mine[at][...] = done
            elif at in places:
                sib[places[at]][...] = done
            else:
                at = max(at - 3, 0) * half
                rest[:, at : at + half] = done

    r = pl.program_id(0)
    seq = seg_ref.shape[1]
    segs = seg_ref[pl.ds(r // per_batch, 1), :]
    row = lax.broadcasted_iota(jnp.int32, (step, seq), 0) + r % per_batch * step
    col = lax.broadcasted_iota(jnp.int32, (step, seq), 1)
    own = jnp.sum(jnp.where(row == col, segs, 0), axis=1, keepdims=True)
    position = jnp.sum(
        jnp.where((own == segs) & (col < row), 1, 0), axis=1, keepdims=True
    )
    lane = lax.broadcasted_iota(jnp.int32, (1, HEAD), 1)
    second = lane >= HEAD // 2
    freq = (lane % (HEAD // 2)).astype(F32)
    angle = position.astype(F32) * jnp.exp(freq * (-2.0 * math.log(1000000.0) / HEAD))
    pair = jnp.cos(angle - jnp.where(second, math.pi / 2, 0.0).astype(F32))
    swapped = pltpu.roll(pair, HEAD // 2, 1)
    cosine = jnp.where(second, swapped, pair)
    sine = jnp.where(second, -pair, swapped)
    cos_ref[...] = cosine
    sin_ref[...] = sine
    for h in range(KVH):
        cols = slice(h * HEAD, (h + 1) * HEAD)
        dproj_ref[:, cols] = turn(cot_ref[:, cols].astype(F32), cosine, sine).astype(BF16)


def prepared(x, gain, segs, cotangent, at):
    rows, wide = x.shape
    step = 256
    half = wide // 16
    outs = [(half, BF16)] * 12 + [(4 * half, BF16), (HEAD, F32), (HEAD, F32), (KW, BF16)]
    def whole(v):
        return pl.BlockSpec(v.shape, lambda r, at: (0, 0))

    def some(n):
        return pl.BlockSpec((step, n), lambda r, at: (r, 0))

    x, gain, segs, cotangent = (
        pltpu.with_memory_space_constraint(v, pltpu.HBM)
        for v in (x, gain[None, :], segs, cotangent)
    )
    return pl.pallas_call(
        functools.partial(prepare_body, segs.shape[1] // step),
        grid_spec=pltpu.PrefetchScalarGridSpec(
            num_scalar_prefetch=1,
            grid=(rows // step,),
            in_specs=[some(wide), whole(gain), whole(segs), some(KW)],
            out_specs=[
                *(some(n) for n, _ in outs),
                pl.BlockSpec((1, 2 * half), lambda r, at: (0, 0)),
            ],
        ),
        out_shape=[
            *(jax.ShapeDtypeStruct((rows, n), t) for n, t in outs),
            jax.ShapeDtypeStruct((1, 2 * half), F32),
        ],
        cost_estimate=pl.CostEstimate(flops=1, bytes_accessed=1, transcendentals=0),
        compiler_params=pltpu.CompilerParams(vmem_limit_bytes=30 * 1024 * 1024),
        name="prepare",
    )(at, x, gain, segs, cotangent)


def keys_body(here, upper, middle, lower, bias, cos_ref, sin_ref, out_ref):
    for h in range(KVH):
        cols = slice(h * HEAD, (h + 1) * HEAD)
        there = jnp.concatenate([v[:, cols] for v in (upper, middle, lower)], axis=0).astype(F32)
        v = here[:, cols] + there + bias[:, cols]
        out_ref[:, cols] = turn(v, cos_ref[...], -sin_ref[...]).astype(BF16)


def product(mine, sib, dproj, dproj_sib):
    dims = (((0,), (0,)), ((), ()))
    return lax.dot_general(mine, dproj, dims, preferred_element_type=F32) + lax.dot_general(
        sib, dproj_sib, dims, preferred_element_type=F32
    )


def spread(rows, chip, outs):
    to_x, to_y, keep_y, keep_x = outs
    half = rows.shape[0] // 2
    low = {1: (to_x, 0), 3: (to_x, half), 2: (keep_y, 0)}[chip]
    high = {2: (to_y, 0), 3: (to_y, half), 1: (keep_x, 0)}[chip]
    for (ref, at), part in ((low, rows[:half]), (high, rows[half:])):
        ref[at : at + half] = part.astype(ref.dtype)


def first_grad_body(m1, m2, m3, s1, s2, s3, dproj, upper, middle, lower, *outs):
    dproj_sib = jnp.concatenate([upper[...], middle[...], lower[...]], axis=0)
    for chip, mine, sib in ((3, m3, s3), (1, m1, s1), (2, m2, s2)):
        spread(product(mine[...], sib[...], dproj[...], dproj_sib), chip, outs)


def second_grad_body(m_a0, m0, m1, m2, m3, s3, rest, dproj, upper, middle, lower, own_a, own_b, *outs):
    dproj_sib = jnp.concatenate([upper[...], middle[...], lower[...]], axis=0)
    half = m0.shape[1]
    own_a[...] = product(m_a0[...], rest[:, :half], dproj[...], dproj_sib)
    for chip, mine in ((3, m3), (1, m1), (2, m2), (0, m0)):
        sib = s3[...] if chip == 3 else rest[:, (chip + 1) * half : (chip + 2) * half]
        rows = product(mine[...], sib, dproj[...], dproj_sib)
        if chip:
            spread(rows, chip, outs)
        else:
            own_b[...] = rows


def forward_body(places, n_acts, n_init, *refs):
    acts, init, refs = refs[:n_acts], refs[n_acts : n_acts + n_init], refs[n_acts + n_init :]
    half = acts[0].shape[1]
    n_outs = 4 if n_init else 2
    weights, outs = refs[:-n_outs], refs[-n_outs:]
    totals = [v[...] for v in init] if n_init else [None, None]
    for side in (1, 0):
        total = totals[side]
        for mine, sib, col, pieces in places:
            w = jnp.concatenate([weights[n][at : at + rows] for n, at, rows in pieces], axis=0)
            rows = acts[sib][:, col * half : (col + 1) * half] if side else acts[mine][...]
            add = jnp.dot(rows, w, preferred_element_type=F32)
            total = add if total is None else total + add
        if side and n_init:
            start = 0
            for out in outs[1:]:
                stop = start + out.shape[0]
                out[...] = total[start:stop].astype(BF16)
                start = stop
        else:
            outs[side][...] = total


def forward(acts, places, weights, init=()):
    tok, kw = acts[0].shape[0], weights[0].shape[1]
    shape = jax.ShapeDtypeStruct((tok, kw), F32)
    third = tok // 48 * 16
    parts = [jax.ShapeDtypeStruct((n, kw), BF16) for n in (third, third, tok - 2 * third)]
    return call(
        functools.partial(forward_body, places, len(acts), len(init)),
        [shape, *parts] if init else [shape, shape],
        "forward",
    )(*acts, *init, *weights)


def collect_body(scale, at_ref, here, over_x, over_y, over_xy, gains_ref, bias_ref):
    n = gains_ref.shape[0] // 8
    chip, core = at_ref[0] // 2, at_ref[0] % 2
    refs = (here, over_x, over_y, over_xy)
    for away, ref in enumerate(refs):
        first = (chip ^ away) * 2
        gains_ref[pl.ds(pl.multiple_of((first + core) * n, n), n)] = ref[:n] * scale
        gains_ref[pl.ds(pl.multiple_of((first + 1 - core) * n, n), n)] = ref[n : 2 * n] * scale
    bias = [ref[2 * n :] for ref in refs]
    bias_ref[...] = ((bias[0] + bias[1]) + (bias[2] + bias[3])) * scale


def by_permutes(hidden_in, segment_ids, key_weight, norm_gain, key_bias, key_cotangent):
    tok = hidden_in.shape[0]
    me = lax.axis_index("blk")
    own, kw = key_weight.shape
    half = own // 2
    quarter = own // 4

    def over(bit):
        return lambda v: lax.ppermute(v, "blk", [(i, i ^ bit) for i in range(8)])

    core, px, py = over(1), over(2), over(4)

    def widen(v):
        return v.astype(F32)

    odd = (lax.axis_index("dp") & 1) == 1
    at = me.reshape(1).astype(jnp.int32)
    odd, at, key_weight, hidden_in, key_cotangent, segment_ids = after(
        (odd, at, key_weight, hidden_in, key_cotangent, segment_ids)
    )
    early = half + own * 3 // 16
    late = own - early
    w_x, w_y = px(key_weight[late:]), py(key_weight[:early])

    parts = prepared(hidden_in, norm_gain, segment_ids, key_cotangent, at)
    mine_a, mine_b, (s_a3, s_a1, s_a2, s_b3, rest) = parts[:4], parts[4:8], parts[8:13]
    cosine, sine, dproj, my_gain = parts[13:]
    my_gain = my_gain.reshape(own)
    third = tok // 48 * 16
    cuts = (0, third, 2 * third, tok)
    dproj_sib = [core(dproj[i:j]) for i, j in zip(cuts[:-1], cuts[1:], strict=True)]
    s_a3, s_a1, s_a2 = core(s_a3), core(s_a1), core(s_a2)

    def part_shapes(h):
        shapes = ((2 * h, BF16), (2 * h, BF16), (h, BF16), (h, BF16))
        return [jax.ShapeDtypeStruct((r, kw), t) for r, t in shapes]

    def add_up(part, from_x, from_y):
        _, _, keep_y, keep_x = part
        more_y = (widen(keep_y) + widen(from_x[quarter:])).astype(BF16)
        more_x = (widen(keep_x) + widen(from_y[quarter:])).astype(BF16)
        return more_y, more_x

    def own_rows(mine, first, second):
        low = mine[:quarter] + widen(first[0][:quarter]) + widen(second[0])
        high = mine[quarter:] + widen(first[1][:quarter]) + widen(second[1])
        return low, high

    def over_z(bit):
        return lambda v: lax.ppermute(v, "dp", [(i, i ^ bit) for i in range(4)])

    def in_pair(low, high):
        sent = jnp.where(odd, low, high).astype(BF16)
        return over_z(1)(sent)

    def pair_sum(low, high, into):
        return (jnp.where(odd, high, low) + widen(into)).astype(BF16)

    def total_of(pair, other):
        return (widen(pair) + widen(other)).astype(BF16)

    def both(total, got):
        return widen(jnp.where(odd, got, total)), widen(jnp.where(odd, total, got))

    part_a = call(first_grad_body, part_shapes(quarter), "grad_a")(
        *mine_a[1:], s_a1, s_a2, s_a3, dproj, *dproj_sib
    )
    to_a = after((part_a[0], part_a[1]), w_x, w_y)
    in_a = px(to_a[0]), py(to_a[1])
    s_b3, rest = after((s_b3, rest), part_a, w_x, w_y)
    s_b3, rest = core(s_b3), core(rest)
    own_shape = jax.ShapeDtypeStruct((half, kw), F32)
    own_a, own_b, *part_b = call(
        second_grad_body, [own_shape, own_shape, *part_shapes(quarter)], "grad_b"
    )(mine_a[0], *mine_b, s_b3, rest, dproj, *dproj_sib)

    acts = (mine_a[0], mine_b[0], mine_a[2], mine_b[1], s_a2, rest)
    places = (
        (0, 5, 0, ((0, 0, half),)),
        (1, 5, 1, ((0, half, half),)),
        (2, 4, 0, ((1, 0, half),)),
        (3, 5, 2, ((2, early - half, half),)),
    )
    here = forward(acts, places, (after(key_weight, part_b), w_y, w_x))

    in_a = after(in_a, here)
    to_b = after((part_b[0], part_b[1]), in_a)
    more = add_up(part_a, *in_a)
    two_a = py(more[0]), px(more[1])
    in_b = px(to_b[0]), py(to_b[1])
    local_a = own_rows(own_a, in_a, two_a)
    pair_a = pair_sum(*local_a, in_pair(*local_a))

    in_b = after(in_b, two_a)
    more = add_up(part_b, *in_b)
    two_b = py(more[0]), px(more[1])
    w_y, w_x, key_weight = after((w_y, w_x, key_weight), two_b)
    more_wx = px(jnp.concatenate([key_weight[:late], w_y[:half]], axis=0))
    more_wy = py(jnp.concatenate([key_weight[early:], w_x[early - half :]], axis=0))
    total_a = total_of(pair_a, over_z(2)(pair_a))
    got_a = over_z(1)(total_a)
    local_b = after(own_rows(own_b, in_b, two_b), total_a)
    into_b = in_pair(*local_b)

    gain_rows = jnp.concatenate(
        [
            jnp.sum(v * widen(key_weight[n * quarter : (n + 1) * quarter]), axis=1)
            for n, v in enumerate((*local_a, *local_b))
        ]
    )
    bias = sum(jnp.sum(widen(v), axis=0) for v in (dproj, *dproj_sib))
    n_own = own // HEAD
    small = jnp.concatenate([gain_rows / my_gain, bias]).reshape(-1, HEAD)
    small = small + over_z(1)(small)
    into_b, small = after((into_b, small))
    pair_b = pair_sum(*local_b, into_b)
    small = small + over_z(2)(small)
    acts = (mine_a[3], mine_b[3], mine_a[1], mine_b[2], s_a3, s_b3, s_a1, rest)
    places = (
        (0, 4, 0, ((0, late, half),)),
        (1, 5, 0, ((1, late, half),)),
        (2, 6, 0, ((0, 0, late), (3, 0, half - late))),
        (3, 7, 3, ((2, half, early - half), (1, 0, late))),
    )
    gains, bias = small[:n_own], small[n_own:]
    other_gains = core(gains)
    other_b, got_a, gains, bias, other_gains, more_wx, more_wy = after(
        (over_z(2)(pair_b), got_a, gains, bias, other_gains, more_wx, more_wy)
    )
    total_b = total_of(pair_b, other_b)
    got_b = over_z(1)(total_b)
    more_wx, more_wy = after((more_wx, more_wy), total_b)
    forwarded = forward(acts, places, (more_wx, more_wy, w_y, w_x), here)

    here, *there = forwarded
    keys = call(keys_body, jax.ShapeDtypeStruct((tok, kw), BF16), "keys")(
        here, *(core(v) for v in there), key_bias[None, :], cosine, sine
    )

    scale = 1.0 / math.sqrt(tok * 32)
    packed = jnp.concatenate([gains, other_gains, bias], axis=0)
    gains, bias = call(
        functools.partial(collect_body, scale),
        [
            jax.ShapeDtypeStruct((8 * n_own, HEAD), F32),
            jax.ShapeDtypeStruct(bias.shape, F32),
        ],
        "collect",
        [pl.BlockSpec(memory_space=pltpu.SMEM)] + [pl.BlockSpec(memory_space=pltpu.VMEM)] * 4,
    )(at, packed, px(packed), py(packed), over(6)(packed))

    got_b, keys = after((got_b, keys))
    grad = jnp.concatenate([*both(total_a, got_a), *both(total_b, got_b)], axis=0)
    return (keys, grad * scale, bias.reshape(-1), gains.reshape(-1))


def by_collectives(hidden_in, segment_ids, key_weight, norm_gain, key_bias, key_cotangent):
    tok_rows = hidden_in.shape[0]
    n_cycle = lax.axis_size("blk")
    n_rep = lax.axis_size("dp")
    positions = positions_of(segment_ids).reshape(tok_rows)
    xf = hidden_in.astype(F32)
    normed = xf * lax.rsqrt(jnp.mean(xf * xf, axis=1, keepdims=True) + 1e-06)
    scaled = (normed * norm_gain[None, :]).astype(BF16)
    cosine, sine = angles_of(positions, HEAD)
    dproj = rotate(key_cotangent.astype(F32), cosine, sine, -1.0).astype(BF16)
    full_weight = lax.all_gather(key_weight, "blk", axis=0, tiled=True)
    projected = jnp.dot(scaled, full_weight, preferred_element_type=F32)
    dscaled = lax.dot_general(
        dproj, full_weight, (((1,), (1,)), ((), ())), preferred_element_type=F32
    )
    projected = projected + key_bias[None, :]
    keys = rotate(projected, cosine, sine, 1.0).astype(BF16)
    cycle_part = lax.psum_scatter(
        lax.dot_general(scaled, dproj, (((0,), (0,)), ((), ())), preferred_element_type=F32),
        "blk",
        scatter_dimension=0,
        tiled=True,
    )
    grad_weight = lax.psum(cycle_part, "dp")
    bias_part = jnp.sum(dproj.astype(F32), axis=0)
    gain_part = jnp.sum(dscaled * normed, axis=0)
    grad_bias, grad_gain = lax.psum((bias_part, gain_part), ("blk", "dp"))
    scale = 1.0 / jnp.sqrt(F32(tok_rows * n_cycle * n_rep))
    return (keys, grad_weight * scale, grad_bias * scale, grad_gain * scale)


def solution(mesh):
    small = mesh.shape["blk"] == 8 and mesh.shape["dp"] == 4
    return jax.shard_map(
        by_permutes if small else by_collectives,
        mesh=mesh,
        in_specs=(
            P(("blk", "dp"), None),
            P(("blk", "dp"), None),
            P("blk", None),
            P(),
            P(),
            P(("blk", "dp"), None),
        ),
        out_specs=(P(("blk", "dp"), None), P("blk", None), P(), P()),
        check_vma=False,
    )
```
